128 devices in a mesh: stretch: 32 (over x, y, core), section: 4 (over z).
Axes of the slice: x: 4, y: 4, z: 4, core: 2. Of those that a mesh axis runs over, the one named last changes fastest.
Arguments:
- latents: bfloat16 [4096, 3072], P('stretch'), may hold values from -6 to 6
- noise_levels: int32 [32], replicated, may hold values from 0 to 15
- frame_lengths: int32 [32], replicated, may hold values from 32 to 128, as said below
- kv_weight: bfloat16 [4, 3072, 1024], P('section'), may hold values from -2 to 2
- mod_shift: float32 [4, 16, 3072], P('section'), may hold values from -3 to 3
- mod_scale: float32 [4, 16, 3072], P('section'), may hold values from -0.5 to 0.5
- mod_gate: float32 [4, 16, 3072], P('section'), may hold values from 0.5 to 2
Outputs:
- hidden: bfloat16 [4, 4096, 3072], P('section', 'stretch')
The draws below stay inside these ranges and needn't reach their ends.
Inputs may be any that keep to these rules, and one draw needn't show every extreme that they name: `frame_lengths`: some video block has all 128 tokens valid.
All inputs are finite; a program needn't handle non-finite values.
Results may differ from the reference program's by a relative error of at most 0.017.
Values may be sent and summed in bfloat16 or wider, within the bound.
A program may use at most 192 MiB of HBM per device.

```python
import math
import jax
import jax.numpy as jnp
from jax import lax

HEAD = 128
HEADS = 24
KV_HEADS = 4
LEVELS = 16
TOK = 128
D = 3072
KVW = 512
BLOCKS = 32
LAYERS = 4
TOKENS = 4096


def draw_latents(key, part):
    key = jax.random.fold_in(key, 11)
    drawn_key = jax.random.fold_in(key, 0)
    return jax.random.truncated_normal(drawn_key, -6.0, 6.0, (TOKENS, D), jnp.float32).astype(jnp.bfloat16)


def draw_kv_weight(key, part):
    key = jax.random.fold_in(key, 13)
    drawn = jax.random.truncated_normal(key, -6.0, 6.0, (LAYERS, D, 2 * KVW), jnp.float32) / math.sqrt(D)
    return drawn.astype(jnp.bfloat16)


def draw_frame_lengths(key, part):
    key = jax.random.fold_in(key, 7)
    first_key, second_key = jax.random.split(key)
    base_lengths = jax.random.randint(first_key, (BLOCKS,), TOK // 4, TOK + 1)
    full_block = jax.random.randint(second_key, (), 0, BLOCKS)
    return jnp.where(jnp.arange(BLOCKS) == full_block, TOK, base_lengths).astype(jnp.int32)


def touch_ends(values, rng, smallest, largest):
    spot = [jax.random.randint(jax.random.fold_in(rng, axis), (), 0, length) for axis, length in enumerate(values.shape)]
    main_axis = values.shape.index(max(values.shape))
    next_to = spot[:main_axis] + [(spot[main_axis] + 1) % values.shape[main_axis]] + spot[main_axis + 1:]
    return values.at[tuple(spot)].set(smallest).at[tuple(next_to)].set(largest)


def block_scale(key, dims, pieces, smallest, largest):
    level = 1.0
    for dim, shards_of in pieces:
        draws = jax.random.uniform(jax.random.fold_in(jax.random.fold_in(key, 6), dim), (shards_of,), jnp.float32, smallest / len(pieces), largest / len(pieces))
        level = level * jnp.repeat(jnp.exp(draws), dims[dim] // shards_of).reshape((-1,) + (1,) * (len(dims) - 1 - dim))
    return level


def scatter_about(own_key, extent, deviation, reach, pieces=(), held_as=jnp.bfloat16):
    drawn = deviation * jax.random.normal(own_key, extent, jnp.float32)
    if pieces:
        drawn = drawn * block_scale(own_key, extent, pieces, -0.22, 0.18)
    return jnp.clip(drawn, -reach, reach).astype(held_as)


def setup_inputs(seed: int = 0) -> dict:
    streams_of = jax.random.split(jax.random.key(seed), 8)
    latents = draw_latents(jax.random.fold_in(streams_of[7], 71), 0)
    noise_levels = touch_ends(jax.random.randint(streams_of[1], (BLOCKS,), 0, LEVELS), jax.random.fold_in(streams_of[1], 1), 0, LEVELS - 1).astype(jnp.int32)
    frame_lengths = draw_frame_lengths(jax.random.fold_in(streams_of[7], 71), 0)
    kv_weight = draw_kv_weight(jax.random.fold_in(streams_of[7], 71), 0)
    mod_shift = scatter_about(streams_of[4], (LAYERS, LEVELS, D), 0.5, 3.0, ((0, 4),), jnp.float32)
    mod_scale = jnp.clip(jax.random.uniform(streams_of[5], (LAYERS, LEVELS, D), jnp.float32, -0.5, 0.5) * block_scale(streams_of[5], (LAYERS, LEVELS, D), ((0, 4),), -0.4, 0.0), -0.5, 0.5)
    mod_gate = jnp.clip(0.5 + 1.5 * jax.random.uniform(streams_of[6], (LAYERS, LEVELS, D), jnp.float32) ** block_scale(streams_of[6], (LAYERS, LEVELS, D), ((0, 4),), -0.2, 0.2), 0.5, 2.0)
    return {"latents": latents, "noise_levels": noise_levels, "frame_lengths": frame_lengths, "kv_weight": kv_weight, "mod_shift": mod_shift, "mod_scale": mod_scale, "mod_gate": mod_gate}


def layer_norm(values):
    row_mean = lax.optimization_barrier(jnp.mean(values, axis=-1, keepdims=True))
    row_var = lax.optimization_barrier(jnp.mean((values - row_mean) ** 2, axis=-1, keepdims=True))
    return (values - row_mean) * lax.rsqrt(row_var + 1e-06)

def reference(latents, noise_levels, frame_lengths, kv_weight, mod_shift, mod_scale, mod_gate):
    head_group = HEADS // KV_HEADS
    kv_width = KV_HEADS * HEAD
    positions = jnp.arange(TOKENS, dtype=jnp.int32)
    key_owner = positions // TOK
    key_live = positions % TOK < frame_lengths[key_owner]
    token_level = noise_levels[key_owner]
    current = latents
    layer_outs = []
    for layer_idx in range(LAYERS):
        shift_rows = mod_shift[layer_idx][token_level]
        scale_rows = mod_scale[layer_idx][token_level]
        gate_rows = mod_gate[layer_idx][token_level]
        normed = (layer_norm(current.astype(jnp.float32)) * (1.0 + scale_rows) + shift_rows).astype(jnp.bfloat16)
        keys_vals = jnp.dot(normed, kv_weight[layer_idx], preferred_element_type=jnp.float32).astype(jnp.bfloat16)
        keys_all = keys_vals[:, :kv_width].reshape(TOKENS, KV_HEADS, HEAD).astype(jnp.float32)
        values_all = keys_vals[:, kv_width:].reshape(TOKENS, KV_HEADS, HEAD).astype(jnp.float32)
        queries = normed.reshape(BLOCKS, TOK, KV_HEADS, head_group, HEAD)

        def one_block(packed):
            query_block, block_idx = packed
            scores = jnp.einsum('tkgd,skd->kgts', query_block.astype(jnp.float32), keys_all, precision=lax.Precision.HIGHEST) / math.sqrt(HEAD)
            allowed = (key_owner <= block_idx) & key_live
            masked = jnp.where(allowed, scores, -1e+30)
            row_top = lax.optimization_barrier(jnp.max(masked, axis=-1, keepdims=True))
            expons = jnp.where(allowed, jnp.exp(masked - row_top), 0.0)
            weights = expons / lax.optimization_barrier(jnp.sum(expons, axis=-1, keepdims=True))
            mixed = jnp.einsum('kgts,skd->tkgd', weights, values_all, precision=lax.Precision.HIGHEST)
            return mixed.reshape(TOK, HEADS * HEAD)
        attended = lax.map(one_block, (queries, jnp.arange(BLOCKS, dtype=jnp.int32))).reshape(TOKENS, HEADS * HEAD)
        current = (current.astype(jnp.float32) + gate_rows * attended).astype(jnp.bfloat16)
        layer_outs.append(current)
    return jnp.stack(layer_outs)
```

```python
import math

import jax
import jax.numpy as jnp
from jax import lax
from jax.experimental import pallas as pl
from jax.experimental.pallas import tpu as pltpu
from jax.sharding import PartitionSpec as P

HEAD = 128
TOK = 128
GRID = 4
SECTIONS = 4
LAYERS = 4
BLOCKS = 2 * GRID * GRID
D = 3072
SLICE = D // SECTIONS
GROUP = SLICE // HEAD
KVW = SECTIONS * HEAD
PIECE = SLICE // (GRID * GRID)
PROWS = TOK + 16
MESH = pl.DeviceIdType.MESH
QSCALE = math.log2(math.e) / math.sqrt(HEAD)
F32 = jnp.float32
BF16 = jnp.bfloat16


def split_two(row):
    high = row.astype(BF16).astype(F32)
    return high, row - high


def stack_rows(rows, width):
    index = lax.broadcasted_iota(jnp.int32, (16, width), 0)
    out = jnp.zeros((16, width), F32)
    for i, row in enumerate(rows):
        out = jnp.where(index == i, row, out)
    return out


def kernel(levels, lengths, latents, weight, shift_tab, scale_tab, gate_tab, out,
           kvbuf, wbuf, w0buf, ybuf, psend, pbuf, statbuf, mods_own, mods, hbuf, qbuf, maskbuf, mbuf, accbuf, kv0,
           s_kvr, s_kvown, s_kvrelay, s_kvsib, s_wzr, s_wzs, s_wloc, s_w1r, s_w1s, s_w2r, s_w2s, s_w3r, s_w3s,
           s_mods, s_modr, s_sts, s_str, s_ps, s_pr, s_kv0, s_outs, s_outr, s_w0):
    c = lax.axis_index("stretch")
    s = lax.axis_index("section")
    core = lax.rem(c, 2)
    chip = c // 2
    x = chip // GRID
    y = lax.rem(chip, GRID)

    def device(xx, yy, kk):
        return (xx * GRID + yy) * 2 + kk

    def remote(src, dst, send, recv, stretch, section):
        return pltpu.make_async_remote_copy(src_ref=src, dst_ref=dst, send_sem=send, recv_sem=recv,
                                            device_id=(stretch, section), device_id_type=MESH)

    def arrived(ref, sem):
        pltpu.make_async_copy(ref, ref, sem).wait()

    barrier = pltpu.get_barrier_semaphore()
    partners = []
    for d in range(1, 4):
        partners.append((c, lax.rem(s + d, SECTIONS)))
        partners.append((device(lax.rem(x + d, GRID), y, core), s))
        partners.append((device(x, lax.rem(y + d, GRID), core), s))
    partners.append((device(x, y, 1 - core), s))
    for partner in partners:
        pl.semaphore_signal(barrier, inc=1, device_id=partner, device_id_type=MESH)

    @pl.when(s == 0)
    def _():
        for i in range(4):
            rows = pl.ds(i * SLICE, SLICE)
            pltpu.make_async_copy(weight.at[0, rows], w0buf.at[rows], s_w0.at[i]).start()

    wown = lax.max(s - 1, 0)

    def own_weight(half):
        return pltpu.make_async_copy(
            weight.at[0, pl.ds(pl.multiple_of(s * SLICE, SLICE), SLICE), pl.ds(half * KVW, KVW)],
            wbuf.at[wown, half], s_wloc.at[half])

    @pl.when(s > 0)
    def _():
        own_weight(0).start()
        own_weight(1).start()

    level = levels[c]
    mods_own[0:1, :] = 1.0 + scale_tab[0, pl.ds(level, 1), :]
    mods_own[1:2, :] = shift_tab[0, pl.ds(level, 1), :]
    mods_own[2:3, :] = gate_tab[0, pl.ds(level, 1), :]
    mods_own[3:8, :] = jnp.zeros((5, D), F32)
    for t in range(SECTIONS):
        @pl.when(s == t)
        def _(t=t):
            mods[t] = mods_own[:, t * SLICE:(t + 1) * SLICE]

    pl.semaphore_wait(barrier, len(partners))

    def mods_copy(t):
        return remote(mods_own.at[:, pl.ds(t * SLICE, SLICE)], mods.at[s], s_mods.at[t], s_modr.at[s], c, t)

    line = jnp.where(core == 0, y * GRID + x, x * GRID + y)
    line_start = jnp.where(core == 0, y * GRID, x * GRID)
    piece_rows = pl.ds(pl.multiple_of(line * PIECE, PIECE), PIECE)

    def wz_copy(t):
        rows = pl.ds(pl.multiple_of(t * SLICE + line * PIECE, PIECE), PIECE)
        columns = pl.ds(pl.multiple_of(core * KVW, KVW), KVW)
        return remote(weight.at[0, rows, columns], wbuf.at[wown, core, piece_rows], s_wzs.at[t], s_wzr.at[wown], c, t)

    for d in range(1, 4):
        t = lax.rem(s + d, SECTIONS)
        mods_copy(t).start()

        @pl.when(s > 0)
        def _(t=t):
            wz_copy(t).start()

    def along_a(d):
        return device(jnp.where(core == 0, lax.rem(x + d, GRID), x), jnp.where(core == 0, y, lax.rem(y + d, GRID)), core)

    def along_b(d):
        return device(jnp.where(core == 0, x, lax.rem(x + d, GRID)), jnp.where(core == 0, lax.rem(y + d, GRID), y), core)

    place_a = jnp.where(core == 0, x, y)
    place_b = jnp.where(core == 0, y, x)
    line_rows = pl.ds(pl.multiple_of(line_start * PIECE, GRID * PIECE), GRID * PIECE)

    def w1_copy(w, d):
        ref = wbuf.at[w, core, piece_rows]
        return remote(ref, ref, s_w1s.at[w, d - 1], s_w1r.at[w, place_a], along_a(d), s)

    def w2_copy(w, d):
        ref = wbuf.at[w, core, line_rows]
        return remote(ref, ref, s_w2s.at[w, d - 1], s_w2r.at[w, place_b], along_b(d), s)

    def w3_copy(w):
        ref = wbuf.at[w, core]
        return remote(ref, ref, s_w3s.at[w], s_w3r.at[w], device(x, y, 1 - core), s)

    def w_step_a(w):
        @pl.when(s != w + 1)
        def _():
            arrived(wbuf.at[w, core, piece_rows], s_wzr.at[w])
            for d in range(1, 4):
                w1_copy(w, d).start()

    def w_step_b(w):
        @pl.when(s != w + 1)
        def _():
            for d in range(1, 4):
                place = lax.rem(place_a + d, GRID)
                rows = pl.ds(pl.multiple_of((line_start + place) * PIECE, PIECE), PIECE)
                arrived(wbuf.at[w, core, rows], s_w1r.at[w, place])
            for d in range(1, 4):
                w2_copy(w, d).start()

    def w_step_c(w):
        @pl.when(s != w + 1)
        def _():
            for d in range(1, 4):
                place = lax.rem(place_b + d, GRID)
                rows = pl.ds(pl.multiple_of(place * GRID * PIECE, GRID * PIECE), GRID * PIECE)
                arrived(wbuf.at[w, core, rows], s_w2r.at[w, place])
            w3_copy(w).start()

    def w_step_d(w):
        @pl.when(s != w + 1)
        def _():
            arrived(wbuf.at[w, 1 - core], s_w3r.at[w])

        @pl.when(s == w + 1)
        def _():
            own_weight(0).wait()
            own_weight(1).wait()

    my_length = lengths[c]

    def finished(keys, values):
        live = lax.broadcasted_iota(jnp.int32, (TOK, HEAD), 0) < my_length
        keys = jnp.where(live, keys, keys[0:1, :]).astype(BF16)
        values = jnp.where(live, values, 0.0)
        return keys, values.T.astype(BF16)

    def store_queries(unit_rows):
        for g in range(GROUP):
            qbuf[g * TOK:(g + 1) * TOK, :] = unit_rows[:, g * HEAD:(g + 1) * HEAD]

    floats = latents[...].astype(F32)
    row_mean = jnp.mean(floats, axis=-1, keepdims=True)
    row_var = jnp.mean((floats - row_mean) ** 2, axis=-1, keepdims=True)
    row_scale = lax.rsqrt(row_var + 1e-06)

    def kv0_copy(t):
        return remote(kv0.at[t], kvbuf.at[0, c], s_kv0.at[t], s_kvr.at[0, c], c, t)

    @pl.when(s == 0)
    def _():
        total = jnp.zeros((TOK, 2 * KVW), F32)
        for i in range(4):
            columns = slice(i * SLICE, (i + 1) * SLICE)
            part = latents[:, columns].astype(F32)
            normed = ((part - row_mean) * row_scale * mods_own[0:1, columns] + mods_own[1:2, columns]).astype(BF16)
            rows = pl.ds(i * SLICE, SLICE)
            pltpu.make_async_copy(weight.at[0, rows], w0buf.at[rows], s_w0.at[i]).wait()
            total = total + jnp.dot(normed, w0buf[i * SLICE:(i + 1) * SLICE, :], preferred_element_type=F32)
        for t in (2, 1, 3, 0):
            keys, values = finished(total[:, t * HEAD:(t + 1) * HEAD], total[:, KVW + t * HEAD:KVW + (t + 1) * HEAD])
            if t == 0:
                kvbuf[0, c, 0:TOK, :] = keys
                kvbuf[0, c, TOK:2 * TOK, :] = values
            else:
                kv0[t, 0:TOK, :] = keys
                kv0[t, TOK:2 * TOK, :] = values
                kv0_copy(t).start()

    for w in range(LAYERS - 1):
        w_step_a(w)

    @pl.when(s != 0)
    def _():
        arrived(mods.at[0], s_modr.at[0])

    my_columns = pl.ds(pl.multiple_of(s * SLICE, SLICE), SLICE)
    part = latents[:, my_columns].astype(F32)
    store_queries((((part - row_mean) * row_scale * mods[0, 0:1, :] + mods[0, 1:2, :]) * QSCALE).astype(BF16))

    def mask_step(j, carry):
        lane = lax.broadcasted_iota(jnp.int32, (16, 2 * TOK), 1)
        limit = jnp.where(lane < TOK, lengths[2 * j], lengths[2 * j + 1] + TOK)
        maskbuf[j] = jnp.where(lane < limit, 1.0, 0.0).astype(BF16)
        return carry

    lax.fori_loop(0, GRID * GRID, mask_step, 0)
    w_step_b(0)

    @pl.when(s != 0)
    def _():
        arrived(kvbuf.at[0, c], s_kvr.at[0, c])

    def kv_copy(l, block, sem, stretch):
        ref = kvbuf.at[l, block]
        return remote(ref, ref, sem, s_kvr.at[l, block], stretch, s)

    def act(copy, begin):
        if begin:
            copy.start()
        else:
            copy.wait_send()

    def own_copies(l, begin):
        @pl.when(core == 0)
        def _():
            act(kv_copy(l, c, s_kvown.at[l, 6], device(x, y, 1)), begin)

        for d in (2, 1, 3):
            @pl.when(x + d < GRID)
            def _(d=d):
                act(kv_copy(l, c, s_kvown.at[l, d - 1], device(x + d, y, core)), begin)

            @pl.when((y + d < GRID) | ((core == 1) & (x < GRID - 1)))
            def _(d=d):
                act(kv_copy(l, c, s_kvown.at[l, 2 + d], device(x, lax.rem(y + d, GRID), core)), begin)

    def row_relays(l, place, begin):
        block = (x * GRID + place) * 2 + 1
        for d in (2, 1, 3):
            @pl.when(x + d < GRID)
            def _(d=d):
                act(kv_copy(l, block, s_kvrelay.at[l, place, d - 1], device(x + d, y, 1)), begin)

    def relays(l, j, begin):
        xx = j // GRID
        yy = lax.rem(j, GRID)
        act(kv_copy(l, 2 * j + core, s_kvsib.at[l, j], device(x, y, 1 - core)), begin)

        @pl.when((core == 0) & (yy == y))
        def _():
            for d in (2, 1, 3):
                act(kv_copy(l, 2 * j, s_kvrelay.at[l, xx, d - 1], device(x, lax.rem(y + d, GRID), 0)), begin)

        @pl.when((core == 1) & (xx == x))
        def _():
            row_relays(l, yy, begin)

    def late_relays(l, begin):
        @pl.when((core == 1) & (x < GRID - 1))
        def _():
            def body(place, carry):
                if begin:
                    block = (x * GRID + place) * 2 + 1
                    arrived(kvbuf.at[l, block], s_kvr.at[l, block])
                row_relays(l, place, begin)
                return carry

            lax.fori_loop(y + 1, GRID, body, 0)

    def pair(first, second, mask):
        keys = jnp.concatenate([first[0:TOK], second[0:TOK]], axis=0)
        values = jnp.concatenate([jnp.concatenate([first[TOK:], second[TOK:]], axis=1), mask], axis=0)
        score = lax.dot_general(keys, qbuf[...], (((1,), (1,)), ((), ())), preferred_element_type=F32)
        old_top = mbuf[0:1, :]
        top = jnp.maximum(old_top, jnp.max(score, axis=0, keepdims=True))
        probs = jnp.exp2(score - top).astype(BF16)
        mbuf[0:1, :] = top
        accbuf[...] = accbuf[...] * jnp.exp2(old_top - top) + jnp.dot(values, probs, preferred_element_type=F32)

    def out_columns():
        return pl.ds(pl.multiple_of(s * SLICE, SLICE), SLICE)

    def out_remote(l):
        return remote(hbuf.at[l], out.at[0, :, out_columns()], s_outs.at[l], s_outr.at[s], c, l)

    def out_local(l):
        return pltpu.make_async_copy(hbuf.at[l], out.at[0, :, out_columns()], s_outs.at[l])

    def p_copy(w, t):
        return remote(psend.at[w, t], pbuf.at[w, s], s_ps.at[w, t], s_pr.at[w, s], c, t)

    def stat_copy(w, t):
        ref = statbuf.at[w, s]
        return remote(ref, ref, s_sts.at[w, t], s_str.at[w, s], c, t)

    def layer(l, carry):
        own_copies(l, True)
        mbuf[...] = jnp.full(mbuf.shape, -1e30, F32)
        accbuf[...] = jnp.zeros(accbuf.shape, F32)

        def step(j, carry):
            arrived(kvbuf.at[l, 2 * j + core], s_kvr.at[l, 2 * j + core])
            relays(l, j, True)
            arrived(kvbuf.at[l, 2 * j + 1 - core], s_kvr.at[l, 2 * j + 1 - core])
            pair(kvbuf[l, 2 * j], kvbuf[l, 2 * j + 1], maskbuf[j])
            return carry

        lax.fori_loop(0, chip, step, 0)

        @pl.when(l < LAYERS - 1)
        def _():
            w_step_c(l)

        @pl.when(l < LAYERS - 2)
        def _():
            w_step_b(l + 1)

        @pl.when(core == 1)
        def _():
            arrived(kvbuf.at[l, 2 * chip], s_kvr.at[l, 2 * chip])

        first = kvbuf[l, 2 * chip]
        second = kvbuf[l, c]
        lane = lax.broadcasted_iota(jnp.int32, (16, 2 * TOK), 1)
        counted = lane < TOK * (1 + core)
        rows = lax.broadcasted_iota(jnp.int32, (2 * TOK, HEAD), 0)
        second = jnp.where(rows < TOK * (1 + core), second, jnp.zeros_like(second))
        pair(first, second, jnp.where(counted, maskbuf[chip], jnp.zeros((16, 2 * TOK), BF16)))

        inverse = 1.0 / accbuf[TOK:TOK + 1, :]
        for g in range(GROUP):
            columns = slice(g * HEAD, (g + 1) * HEAD)
            attended = (accbuf[0:TOK, g * TOK:(g + 1) * TOK] * inverse[:, g * TOK:(g + 1) * TOK]).T

            @pl.when(l == 0)
            def _(g=g, columns=columns):
                start = pl.ds(pl.multiple_of(s * SLICE + g * HEAD, HEAD), HEAD)
                hbuf[0, :, columns] = latents[:, start]

            @pl.when(l > 0)
            def _(columns=columns):
                hbuf[l, :, columns] = hbuf[lax.max(l - 1, 0), :, columns]

            gate = mods[l, 2:3, columns]
            hbuf[l, :, columns] = (hbuf[l, :, columns].astype(F32) + gate * attended).astype(BF16)

        @pl.when(l < LAYERS - 1)
        def _():
            w = l
            hidden = hbuf[l].astype(F32)
            mean = jnp.mean(hidden, axis=-1, keepdims=True)
            centred = hidden - mean
            square = jnp.sum(centred * centred, axis=-1, keepdims=True)
            lane = lax.broadcasted_iota(jnp.int32, (TOK, HEAD), 1)
            tile = jnp.where(lane == 0, mean, jnp.where(lane == 1, square, 0.0)).T
            statbuf[w, s] = tile[0:8, :]
            for d in (2, 1, 3):
                stat_copy(w, lax.rem(s + d, SECTIONS)).start()

            @pl.when(s != l + 1)
            def _():
                arrived(mods.at[l + 1], s_modr.at[l + 1])

            gain = mods[l + 1, 0:1, :]
            shift = mods[l + 1, 1:2, :]
            ybuf[0:TOK, :] = (centred * gain).astype(BF16)
            ybuf[TOK:PROWS, :] = stack_rows(split_two(gain) + split_two(shift), SLICE).astype(BF16)
            w_step_d(w)
            halves = [jnp.dot(ybuf[...], wbuf[w, i], preferred_element_type=F32) for i in range(2)]
            for i in range(2):
                extra = halves[i][TOK:PROWS]
                extra = stack_rows(split_two(extra[0:1] + extra[1:2]) + split_two(extra[2:3] + extra[3:4]), KVW)
                halves[i] = jnp.concatenate([halves[i][0:TOK], extra], axis=0).astype(BF16)
            for t in range(SECTIONS):
                for i in range(2):
                    psend[w, t, :, i * HEAD:(i + 1) * HEAD] = halves[i][:, t * HEAD:(t + 1) * HEAD]
            for d in (2, 1, 3):
                p_copy(w, lax.rem(s + d, SECTIONS)).start()

        @pl.when(s != l)
        def _():
            out_remote(l).start()

        @pl.when(s == l)
        def _():
            out_local(l).start()

        late_relays(l, True)

        @pl.when(l < LAYERS - 1)
        def _():
            w = l
            for d in range(1, 4):
                t = lax.rem(s + d, SECTIONS)
                arrived(statbuf.at[w, t], s_str.at[w, t])
            stats = jnp.concatenate([statbuf[w, t] for t in range(SECTIONS)] + [jnp.zeros((TOK - 8 * SECTIONS, HEAD), F32)], axis=0).T
            means = [stats[:, 8 * t:8 * t + 1] for t in range(SECTIONS)]
            squares = [stats[:, 8 * t + 1:8 * t + 2] for t in range(SECTIONS)]
            mean = sum(means) / SECTIONS
            offsets = [m - mean for m in means]
            variance = sum(sq + SLICE * o * o for sq, o in zip(squares, offsets)) / D
            scale = lax.rsqrt(variance + 1e-06)
            gain = mods[l + 1, 0:1, :]
            shift = mods[l + 1, 1:2, :]
            store_queries((((hbuf[l].astype(F32) - mean) * scale * gain + shift) * QSCALE).astype(BF16))
            pbuf[w, s] = psend[w, s]
            for d in range(1, 4):
                t = lax.rem(s + d, SECTIONS)
                arrived(pbuf.at[w, t], s_pr.at[w, t])
            total = jnp.zeros((TOK, 2 * HEAD), F32)
            bias = jnp.zeros((1, 2 * HEAD), F32)
            for t in range(SECTIONS):
                extra = pbuf[w, t, TOK:PROWS, :].astype(F32)
                total = total + pbuf[w, t, 0:TOK, :].astype(F32) + offsets[t] * (extra[0:1] + extra[1:2])
                bias = bias + extra[2:3] + extra[3:4]
            total = total * scale + bias
            keys, values = finished(total[:, 0:HEAD], total[:, HEAD:])
            kvbuf[l + 1, c, 0:TOK, :] = keys
            kvbuf[l + 1, c, TOK:2 * TOK, :] = values

        return carry

    lax.fori_loop(0, LAYERS, layer, 0)

    def layer_sent(l, carry):
        own_copies(l, False)

        def step(j, carry):
            relays(l, j, False)
            return carry

        lax.fori_loop(0, chip, step, 0)
        late_relays(l, False)

        @pl.when(s != l)
        def _():
            out_remote(l).wait_send()

        return carry

    lax.fori_loop(0, LAYERS, layer_sent, 0)
    out_local(s).wait()
    for d in range(1, 4):
        t = lax.rem(s + d, SECTIONS)
        mods_copy(t).wait_send()

        @pl.when(s > 0)
        def _(t=t):
            wz_copy(t).wait_send()

    @pl.when(s == 0)
    def _():
        for t in range(1, SECTIONS):
            kv0_copy(t).wait_send()

    def plane_sent(w, carry):
        for d in range(1, 4):
            t = lax.rem(s + d, SECTIONS)
            stat_copy(w, t).wait_send()
            p_copy(w, t).wait_send()

        @pl.when(s != w + 1)
        def _():
            for d in range(1, 4):
                w1_copy(w, d).wait_send()
                w2_copy(w, d).wait_send()
            w3_copy(w).wait_send()

        return carry

    lax.fori_loop(0, LAYERS - 1, plane_sent, 0)
    for d in range(1, 4):
        t = lax.rem(s + d, SECTIONS)
        arrived(out.at[0, :, pl.ds(pl.multiple_of(t * SLICE, SLICE), SLICE)], s_outr.at[t])


def shards(latents, noise_levels, frame_lengths, kv_weight, mod_shift, mod_scale, mod_gate):
    dma = pltpu.SemaphoreType.DMA
    smem = pl.BlockSpec(memory_space=pltpu.SMEM)
    vmem = pl.BlockSpec(memory_space=pltpu.VMEM)
    anywhere = pl.BlockSpec(memory_space=pl.ANY)
    wide = LAYERS - 1
    return pl.pallas_call(
        kernel,
        out_shape=jax.ShapeDtypeStruct((1, TOK, D), BF16),
        in_specs=[smem, smem, vmem, anywhere, vmem, vmem, vmem],
        out_specs=anywhere,
        scratch_shapes=[
            pltpu.VMEM((LAYERS, BLOCKS, 2 * TOK, HEAD), BF16),
            pltpu.VMEM((wide, 2, SLICE, KVW), BF16),
            pltpu.VMEM((D, 2 * KVW), BF16),
            pltpu.VMEM((PROWS, SLICE), BF16),
            pltpu.VMEM((wide, SECTIONS, PROWS, 2 * HEAD), BF16),
            pltpu.VMEM((wide, SECTIONS, PROWS, 2 * HEAD), BF16),
            pltpu.VMEM((wide, SECTIONS, 8, HEAD), F32),
            pltpu.VMEM((8, D), F32),
            pltpu.VMEM((LAYERS, 8, SLICE), F32),
            pltpu.VMEM((LAYERS, TOK, SLICE), BF16),
            pltpu.VMEM((SLICE, HEAD), BF16),
            pltpu.VMEM((GRID * GRID, 16, 2 * TOK), BF16),
            pltpu.VMEM((8, SLICE), F32),
            pltpu.VMEM((PROWS, SLICE), F32),
            pltpu.VMEM((SECTIONS, 2 * TOK, HEAD), BF16),
            dma((LAYERS, BLOCKS)), dma((LAYERS, 7)), dma((LAYERS, GRID, 3)), dma((LAYERS, GRID * GRID)),
            dma((wide,)), dma((SECTIONS,)), dma((2,)), dma((wide, GRID)), dma((wide, 3)), dma((wide, GRID)),
            dma((wide, 3)), dma((wide,)), dma((wide,)),
            dma((SECTIONS,)), dma((SECTIONS,)), dma((wide, SECTIONS)), dma((wide, SECTIONS)),
            dma((wide, SECTIONS)), dma((wide, SECTIONS)), dma((SECTIONS,)), dma((LAYERS,)), dma((SECTIONS,)), dma((4,)),
        ],
        compiler_params=pltpu.CompilerParams(
            collective_id=0, has_side_effects=True, vmem_limit_bytes=56 * 1024 * 1024
        ),
    )(noise_levels, frame_lengths, latents, kv_weight, mod_shift, mod_scale, mod_gate)


def solution(mesh):
    in_specs = (
        P("stretch", None),
        P(),
        P(),
        P("section", None, None),
        P("section", None, None),
        P("section", None, None),
        P("section", None, None),
    )
    out_specs = P("section", "stretch", None)
    return jax.shard_map(shards, mesh=mesh, in_specs=in_specs, out_specs=out_specs, check_vma=False)
```

```python
import math

import jax
import jax.numpy as jnp
from jax import lax
from jax.experimental import pallas as pl
from jax.experimental.pallas import tpu as pltpu
from jax.sharding import PartitionSpec as P

HEAD = 128
TOK = 128
GRID = 4
SECTIONS = 4
LAYERS = 4
BLOCKS = 2 * GRID * GRID
D = 3072
SLICE = D // SECTIONS
GROUP = SLICE // HEAD
KVW = SECTIONS * HEAD
PIECE = SLICE // (GRID * GRID)
PROWS = TOK + 16
MESH = pl.DeviceIdType.MESH
QSCALE = math.log2(math.e) / math.sqrt(HEAD)
F32 = jnp.float32
BF16 = jnp.bfloat16


def split_two(row):
    high = row.astype(BF16).astype(F32)
    return high, row - high


def stack_rows(rows, width):
    index = lax.broadcasted_iota(jnp.int32, (16, width), 0)
    out = jnp.zeros((16, width), F32)
    for i, row in enumerate(rows):
        out = jnp.where(index == i, row, out)
    return out


def kernel(levels, lengths, latents, weight, shift_tab, scale_tab, gate_tab, out,
           kvbuf, wbuf, w0buf, ybuf, psend, pbuf, statbuf, mods_own, mods, hbuf, qbuf, maskbuf, mbuf, accbuf, kv0,
           s_kvr, s_kvown, s_kvrelay, s_kvsib, s_wzr, s_wzs, s_wloc, s_w1r, s_w1s, s_w2r, s_w2s, s_w3r, s_w3s,
           s_mods, s_modr, s_sts, s_str, s_ps, s_pr, s_kv0, s_outs, s_outr, s_w0):
    c = lax.axis_index("stretch")
    s = lax.axis_index("section")
    core = lax.rem(c, 2)
    chip = c // 2
    x = chip // GRID
    y = lax.rem(chip, GRID)

    def device(xx, yy, kk):
        return (xx * GRID + yy) * 2 + kk

    def remote(src, dst, send, recv, stretch, section):
        return pltpu.make_async_remote_copy(src_ref=src, dst_ref=dst, send_sem=send, recv_sem=recv,
                                            device_id=(stretch, section), device_id_type=MESH)

    def arrived(ref, sem):
        pltpu.make_async_copy(ref, ref, sem).wait()

    barrier = pltpu.get_barrier_semaphore()
    partners = []
    for d in range(1, 4):
        partners.append((c, lax.rem(s + d, SECTIONS)))
        partners.append((device(lax.rem(x + d, GRID), y, core), s))
        partners.append((device(x, lax.rem(y + d, GRID), core), s))
    partners.append((device(x, y, 1 - core), s))
    for partner in partners:
        pl.semaphore_signal(barrier, inc=1, device_id=partner, device_id_type=MESH)

    @pl.when(s == 0)
    def _():
        for i in range(4):
            rows = pl.ds(i * SLICE, SLICE)
            pltpu.make_async_copy(weight.at[0, rows], w0buf.at[rows], s_w0.at[i]).start()

    wown = lax.max(s - 1, 0)

    def own_weight(half):
        return pltpu.make_async_copy(
            weight.at[0, pl.ds(pl.multiple_of(s * SLICE, SLICE), SLICE), pl.ds(half * KVW, KVW)],
            wbuf.at[wown, half], s_wloc.at[half])

    @pl.when(s > 0)
    def _():
        own_weight(0).start()
        own_weight(1).start()

    level = levels[c]
    mods_own[0:1, :] = 1.0 + scale_tab[0, pl.ds(level, 1), :]
    mods_own[1:2, :] = shift_tab[0, pl.ds(level, 1), :]
    mods_own[2:3, :] = gate_tab[0, pl.ds(level, 1), :]
    mods_own[3:8, :] = jnp.zeros((5, D), F32)
    for t in range(SECTIONS):
        @pl.when(s == t)
        def _(t=t):
            mods[t] = mods_own[:, t * SLICE:(t + 1) * SLICE]

    pl.semaphore_wait(barrier, len(partners))

    def mods_copy(t):
        return remote(mods_own.at[:, pl.ds(t * SLICE, SLICE)], mods.at[s], s_mods.at[t], s_modr.at[s], c, t)

    line = jnp.where(core == 0, y * GRID + x, x * GRID + y)
    line_start = jnp.where(core == 0, y * GRID, x * GRID)
    piece_rows = pl.ds(pl.multiple_of(line * PIECE, PIECE), PIECE)

    def wz_copy(t):
        rows = pl.ds(pl.multiple_of(t * SLICE + line * PIECE, PIECE), PIECE)
        columns = pl.ds(pl.multiple_of(core * KVW, KVW), KVW)
        return remote(weight.at[0, rows, columns], wbuf.at[wown, core, piece_rows], s_wzs.at[t], s_wzr.at[wown], c, t)

    for d in range(1, 4):
        t = lax.rem(s + d, SECTIONS)
        mods_copy(t).start()

        @pl.when(s > 0)
        def _(t=t):
            wz_copy(t).start()

    def along_a(d):
        return device(jnp.where(core == 0, lax.rem(x + d, GRID), x), jnp.where(core == 0, y, lax.rem(y + d, GRID)), core)

    def along_b(d):
        return device(jnp.where(core == 0, x, lax.rem(x + d, GRID)), jnp.where(core == 0, lax.rem(y + d, GRID), y), core)

    place_a = jnp.where(core == 0, x, y)
    place_b = jnp.where(core == 0, y, x)
    line_rows = pl.ds(pl.multiple_of(line_start * PIECE, GRID * PIECE), GRID * PIECE)

    def w1_copy(w, d):
        ref = wbuf.at[w, core, piece_rows]
        return remote(ref, ref, s_w1s.at[w, d - 1], s_w1r.at[w, place_a], along_a(d), s)

    def w2_copy(w, d):
        ref = wbuf.at[w, core, line_rows]
        return remote(ref, ref, s_w2s.at[w, d - 1], s_w2r.at[w, place_b], along_b(d), s)

    def w3_copy(w):
        ref = wbuf.at[w, core]
        return remote(ref, ref, s_w3s.at[w], s_w3r.at[w], device(x, y, 1 - core), s)

    def w_step_a(w):
        @pl.when(s != w + 1)
        def _():
            arrived(wbuf.at[w, core, piece_rows], s_wzr.at[w])
            for d in range(1, 4):
                w1_copy(w, d).start()

    def w_step_b(w):
        @pl.when(s != w + 1)
        def _():
            for d in range(1, 4):
                place = lax.rem(place_a + d, GRID)
                rows = pl.ds(pl.multiple_of((line_start + place) * PIECE, PIECE), PIECE)
                arrived(wbuf.at[w, core, rows], s_w1r.at[w, place])
            for d in range(1, 4):
                w2_copy(w, d).start()

    def w_step_c(w):
        @pl.when(s != w + 1)
        def _():
            for d in range(1, 4):
                place = lax.rem(place_b + d, GRID)
                rows = pl.ds(pl.multiple_of(place * GRID * PIECE, GRID * PIECE), GRID * PIECE)
                arrived(wbuf.at[w, core, rows], s_w2r.at[w, place])
            w3_copy(w).start()

    def w_step_d(w):
        @pl.when(s != w + 1)
        def _():
            arrived(wbuf.at[w, 1 - core], s_w3r.at[w])

        @pl.when(s == w + 1)
        def _():
            own_weight(0).wait()
            own_weight(1).wait()

    my_length = lengths[c]

    def finished(keys, values):
        live = lax.broadcasted_iota(jnp.int32, (TOK, HEAD), 0) < my_length
        keys = jnp.where(live, keys, keys[0:1, :]).astype(BF16)
        values = jnp.where(live, values, 0.0)
        return keys, values.T.astype(BF16)

    def store_queries(unit_rows):
        for g in range(GROUP):
            qbuf[g * TOK:(g + 1) * TOK, :] = unit_rows[:, g * HEAD:(g + 1) * HEAD]

    floats = latents[...].astype(F32)
    row_mean = jnp.mean(floats, axis=-1, keepdims=True)
    row_var = jnp.mean((floats - row_mean) ** 2, axis=-1, keepdims=True)
    row_scale = lax.rsqrt(row_var + 1e-06)

    def kv0_copy(t):
        return remote(kv0.at[t], kvbuf.at[0, c], s_kv0.at[t], s_kvr.at[0, c], c, t)

    @pl.when(s == 0)
    def _():
        total = jnp.zeros((TOK, 2 * KVW), F32)
        for i in range(4):
            columns = slice(i * SLICE, (i + 1) * SLICE)
            part = latents[:, columns].astype(F32)
            normed = ((part - row_mean) * row_scale * mods_own[0:1, columns] + mods_own[1:2, columns]).astype(BF16)
            rows = pl.ds(i * SLICE, SLICE)
            pltpu.make_async_copy(weight.at[0, rows], w0buf.at[rows], s_w0.at[i]).wait()
            total = total + jnp.dot(normed, w0buf[i * SLICE:(i + 1) * SLICE, :], preferred_element_type=F32)
        for t in (2, 1, 3, 0):
            keys, values = finished(total[:, t * HEAD:(t + 1) * HEAD], total[:, KVW + t * HEAD:KVW + (t + 1) * HEAD])
            if t == 0:
                kvbuf[0, c, 0:TOK, :] = keys
                kvbuf[0, c, TOK:2 * TOK, :] = values
            else:
                kv0[t, 0:TOK, :] = keys
                kv0[t, TOK:2 * TOK, :] = values
                kv0_copy(t).start()

    for w in range(LAYERS - 1):
        w_step_a(w)

    @pl.when(s != 0)
    def _():
        arrived(mods.at[0], s_modr.at[0])

    my_columns = pl.ds(pl.multiple_of(s * SLICE, SLICE), SLICE)
    part = latents[:, my_columns].astype(F32)
    store_queries((((part - row_mean) * row_scale * mods[0, 0:1, :] + mods[0, 1:2, :]) * QSCALE).astype(BF16))

    def mask_step(j, carry):
        lane = lax.broadcasted_iota(jnp.int32, (16, 2 * TOK), 1)
        limit = jnp.where(lane < TOK, lengths[2 * j], lengths[2 * j + 1] + TOK)
        maskbuf[j] = jnp.where(lane < limit, 1.0, 0.0).astype(BF16)
        return carry

    lax.fori_loop(0, GRID * GRID, mask_step, 0)
    w_step_b(0)

    @pl.when(s != 0)
    def _():
        arrived(kvbuf.at[0, c], s_kvr.at[0, c])

    def kv_copy(l, block, sem, stretch):
        ref = kvbuf.at[l, block]
        return remote(ref, ref, sem, s_kvr.at[l, block], stretch, s)

    def act(copy, begin):
        if begin:
            copy.start()
        else:
            copy.wait_send()

    def own_copies(l, begin):
        @pl.when(core == 0)
        def _():
            act(kv_copy(l, c, s_kvown.at[l, 6], device(x, y, 1)), begin)

        for d in (2, 1, 3):
            @pl.when(x + d < GRID)
            def _(d=d):
                act(kv_copy(l, c, s_kvown.at[l, d - 1], device(x + d, y, core)), begin)

            @pl.when((y + d < GRID) | ((core == 1) & (x < GRID - 1)))
            def _(d=d):
                act(kv_copy(l, c, s_kvown.at[l, 2 + d], device(x, lax.rem(y + d, GRID), core)), begin)

    def sibling_copy(l, j):
        return kv_copy(l, 2 * j + core, s_kvsib.at[l, j], device(x, y, 1 - core))

    def own_core_arrived(l, j):
        arrived(kvbuf.at[l, 2 * j + core], s_kvr.at[l, 2 * j + core])

    def column_relays(l, begin):
        def body(xx, carry):
            j = xx * GRID + y
            if begin:
                own_core_arrived(l, j)

            @pl.when(core == 0)
            def _():
                for d in (2, 1, 3):
                    act(kv_copy(l, 2 * j, s_kvrelay.at[l, xx, d - 1], device(x, lax.rem(y + d, GRID), 0)), begin)

            act(sibling_copy(l, j), begin)
            return carry

        lax.fori_loop(0, x, body, 0)

    def row_relays(l, begin):
        for e in (1, 3, 2):
            place = lax.rem(y + e, GRID)
            j = x * GRID + place

            @pl.when((place < y) | ((core == 1) & (x < GRID - 1)))
            def _(j=j, place=place):
                if begin:
                    own_core_arrived(l, j)

                @pl.when((core == 1) & (x < GRID - 1))
                def _():
                    for d in (2, 1, 3):
                        @pl.when(x + d < GRID)
                        def _(d=d):
                            act(kv_copy(l, 2 * j + 1, s_kvrelay.at[l, place, d - 1], device(x + d, y, 1)), begin)

                @pl.when(place < y)
                def _():
                    act(sibling_copy(l, j), begin)

    def other_relays(l, xx, begin):
        for e in (1, 3, 2):
            j = xx * GRID + lax.rem(y + e, GRID)
            if begin:
                own_core_arrived(l, j)
            act(sibling_copy(l, j), begin)

    def pair(first, second, mask):
        keys = jnp.concatenate([first[0:TOK], second[0:TOK]], axis=0)
        values = jnp.concatenate([jnp.concatenate([first[TOK:], second[TOK:]], axis=1), mask], axis=0)
        score = lax.dot_general(keys, qbuf[...], (((1,), (1,)), ((), ())), preferred_element_type=F32)
        old_top = mbuf[0:1, :]
        top = jnp.maximum(old_top, jnp.max(score, axis=0, keepdims=True))
        probs = jnp.exp2(score - top).astype(BF16)
        mbuf[0:1, :] = top
        accbuf[...] = accbuf[...] * jnp.exp2(old_top - top) + jnp.dot(values, probs, preferred_element_type=F32)

    def out_columns():
        return pl.ds(pl.multiple_of(s * SLICE, SLICE), SLICE)

    def out_remote(l):
        return remote(hbuf.at[l], out.at[0, :, out_columns()], s_outs.at[l], s_outr.at[s], c, l)

    def out_local(l):
        return pltpu.make_async_copy(hbuf.at[l], out.at[0, :, out_columns()], s_outs.at[l])

    def p_copy(w, t):
        return remote(psend.at[w, t], pbuf.at[w, s], s_ps.at[w, t], s_pr.at[w, s], c, t)

    def stat_copy(w, t):
        ref = statbuf.at[w, s]
        return remote(ref, ref, s_sts.at[w, t], s_str.at[w, s], c, t)

    def layer(l, carry):
        own_copies(l, True)
        mbuf[...] = jnp.full(mbuf.shape, -1e30, F32)
        accbuf[...] = jnp.zeros(accbuf.shape, F32)

        def step(j, carry):
            arrived(kvbuf.at[l, 2 * j + 1 - core], s_kvr.at[l, 2 * j + 1 - core])
            pair(kvbuf[l, 2 * j], kvbuf[l, 2 * j + 1], maskbuf[j])
            return carry

        column_relays(l, True)

        @pl.when((l == 0) | (x == 0))
        def _():
            row_relays(l, True)

        def row(xx, carry):
            other_relays(l, xx, True)
            lax.fori_loop(xx * GRID, (xx + 1) * GRID, step, 0)

            @pl.when((l > 0) & (xx == 0))
            def _():
                row_relays(l, True)

            return carry

        lax.fori_loop(0, x, row, 0)

        @pl.when(l < LAYERS - 1)
        def _():
            w_step_c(l)

        @pl.when(l < LAYERS - 2)
        def _():
            w_step_b(l + 1)

        lax.fori_loop(x * GRID, chip, step, 0)

        @pl.when(core == 1)
        def _():
            arrived(kvbuf.at[l, 2 * chip], s_kvr.at[l, 2 * chip])

        first = kvbuf[l, 2 * chip]
        second = kvbuf[l, c]
        lane = lax.broadcasted_iota(jnp.int32, (16, 2 * TOK), 1)
        counted = lane < TOK * (1 + core)
        rows = lax.broadcasted_iota(jnp.int32, (2 * TOK, HEAD), 0)
        second = jnp.where(rows < TOK * (1 + core), second, jnp.zeros_like(second))
        pair(first, second, jnp.where(counted, maskbuf[chip], jnp.zeros((16, 2 * TOK), BF16)))

        inverse = 1.0 / accbuf[TOK:TOK + 1, :]
        for g in range(GROUP):
            columns = slice(g * HEAD, (g + 1) * HEAD)
            attended = (accbuf[0:TOK, g * TOK:(g + 1) * TOK] * inverse[:, g * TOK:(g + 1) * TOK]).T

            @pl.when(l == 0)
            def _(g=g, columns=columns):
                start = pl.ds(pl.multiple_of(s * SLICE + g * HEAD, HEAD), HEAD)
                hbuf[0, :, columns] = latents[:, start]

            @pl.when(l > 0)
            def _(columns=columns):
                hbuf[l, :, columns] = hbuf[lax.max(l - 1, 0), :, columns]

            gate = mods[l, 2:3, columns]
            hbuf[l, :, columns] = (hbuf[l, :, columns].astype(F32) + gate * attended).astype(BF16)

        @pl.when(l < LAYERS - 1)
        def _():
            w = l
            hidden = hbuf[l].astype(F32)
            mean = jnp.mean(hidden, axis=-1, keepdims=True)
            centred = hidden - mean
            square = jnp.sum(centred * centred, axis=-1, keepdims=True)
            lane = lax.broadcasted_iota(jnp.int32, (TOK, HEAD), 1)
            tile = jnp.where(lane == 0, mean, jnp.where(lane == 1, square, 0.0)).T
            statbuf[w, s] = tile[0:8, :]
            for d in (2, 1, 3):
                stat_copy(w, lax.rem(s + d, SECTIONS)).start()

            @pl.when(s != l + 1)
            def _():
                arrived(mods.at[l + 1], s_modr.at[l + 1])

            gain = mods[l + 1, 0:1, :]
            shift = mods[l + 1, 1:2, :]
            ybuf[0:TOK, :] = (centred * gain).astype(BF16)
            ybuf[TOK:PROWS, :] = stack_rows(split_two(gain) + split_two(shift), SLICE).astype(BF16)
            w_step_d(w)
            halves = [jnp.dot(ybuf[...], wbuf[w, i], preferred_element_type=F32) for i in range(2)]
            for i in range(2):
                extra = halves[i][TOK:PROWS]
                extra = stack_rows(split_two(extra[0:1] + extra[1:2]) + split_two(extra[2:3] + extra[3:4]), KVW)
                halves[i] = jnp.concatenate([halves[i][0:TOK], extra], axis=0).astype(BF16)
            for t in range(SECTIONS):
                for i in range(2):
                    psend[w, t, :, i * HEAD:(i + 1) * HEAD] = halves[i][:, t * HEAD:(t + 1) * HEAD]
            for d in (2, 1, 3):
                p_copy(w, lax.rem(s + d, SECTIONS)).start()

        @pl.when(s != l)
        def _():
            out_remote(l).start()

        @pl.when(s == l)
        def _():
            out_local(l).start()

        @pl.when(l < LAYERS - 1)
        def _():
            w = l
            for d in range(1, 4):
                t = lax.rem(s + d, SECTIONS)
                arrived(statbuf.at[w, t], s_str.at[w, t])
            stats = jnp.concatenate([statbuf[w, t] for t in range(SECTIONS)] + [jnp.zeros((TOK - 8 * SECTIONS, HEAD), F32)], axis=0).T
            means = [stats[:, 8 * t:8 * t + 1] for t in range(SECTIONS)]
            squares = [stats[:, 8 * t + 1:8 * t + 2] for t in range(SECTIONS)]
            mean = sum(means) / SECTIONS
            offsets = [m - mean for m in means]
            variance = sum(sq + SLICE * o * o for sq, o in zip(squares, offsets)) / D
            scale = lax.rsqrt(variance + 1e-06)
            gain = mods[l + 1, 0:1, :]
            shift = mods[l + 1, 1:2, :]
            store_queries((((hbuf[l].astype(F32) - mean) * scale * gain + shift) * QSCALE).astype(BF16))
            pbuf[w, s] = psend[w, s]
            for d in range(1, 4):
                t = lax.rem(s + d, SECTIONS)
                arrived(pbuf.at[w, t], s_pr.at[w, t])
            total = jnp.zeros((TOK, 2 * HEAD), F32)
            bias = jnp.zeros((1, 2 * HEAD), F32)
            for t in range(SECTIONS):
                extra = pbuf[w, t, TOK:PROWS, :].astype(F32)
                total = total + pbuf[w, t, 0:TOK, :].astype(F32) + offsets[t] * (extra[0:1] + extra[1:2])
                bias = bias + extra[2:3] + extra[3:4]
            total = total * scale + bias
            keys, values = finished(total[:, 0:HEAD], total[:, HEAD:])
            kvbuf[l + 1, c, 0:TOK, :] = keys
            kvbuf[l + 1, c, TOK:2 * TOK, :] = values

        return carry

    lax.fori_loop(0, LAYERS, layer, 0)

    def layer_sent(l, carry):
        own_copies(l, False)

        column_relays(l, False)
        row_relays(l, False)

        def row(xx, carry):
            other_relays(l, xx, False)
            return carry

        lax.fori_loop(0, x, row, 0)

        @pl.when(s != l)
        def _():
            out_remote(l).wait_send()

        return carry

    lax.fori_loop(0, LAYERS, layer_sent, 0)
    out_local(s).wait()
    for d in range(1, 4):
        t = lax.rem(s + d, SECTIONS)
        mods_copy(t).wait_send()

        @pl.when(s > 0)
        def _(t=t):
            wz_copy(t).wait_send()

    @pl.when(s == 0)
    def _():
        for t in range(1, SECTIONS):
            kv0_copy(t).wait_send()

    def plane_sent(w, carry):
        for d in range(1, 4):
            t = lax.rem(s + d, SECTIONS)
            stat_copy(w, t).wait_send()
            p_copy(w, t).wait_send()

        @pl.when(s != w + 1)
        def _():
            for d in range(1, 4):
                w1_copy(w, d).wait_send()
                w2_copy(w, d).wait_send()
            w3_copy(w).wait_send()

        return carry

    lax.fori_loop(0, LAYERS - 1, plane_sent, 0)
    for d in range(1, 4):
        t = lax.rem(s + d, SECTIONS)
        arrived(out.at[0, :, pl.ds(pl.multiple_of(t * SLICE, SLICE), SLICE)], s_outr.at[t])


def shards(latents, noise_levels, frame_lengths, kv_weight, mod_shift, mod_scale, mod_gate):
    dma = pltpu.SemaphoreType.DMA
    smem = pl.BlockSpec(memory_space=pltpu.SMEM)
    vmem = pl.BlockSpec(memory_space=pltpu.VMEM)
    anywhere = pl.BlockSpec(memory_space=pl.ANY)
    wide = LAYERS - 1
    return pl.pallas_call(
        kernel,
        out_shape=jax.ShapeDtypeStruct((1, TOK, D), BF16),
        in_specs=[smem, smem, vmem, anywhere, vmem, vmem, vmem],
        out_specs=anywhere,
        scratch_shapes=[
            pltpu.VMEM((LAYERS, BLOCKS, 2 * TOK, HEAD), BF16),
            pltpu.VMEM((wide, 2, SLICE, KVW), BF16),
            pltpu.VMEM((D, 2 * KVW), BF16),
            pltpu.VMEM((PROWS, SLICE), BF16),
            pltpu.VMEM((wide, SECTIONS, PROWS, 2 * HEAD), BF16),
            pltpu.VMEM((wide, SECTIONS, PROWS, 2 * HEAD), BF16),
            pltpu.VMEM((wide, SECTIONS, 8, HEAD), F32),
            pltpu.VMEM((8, D), F32),
            pltpu.VMEM((LAYERS, 8, SLICE), F32),
            pltpu.VMEM((LAYERS, TOK, SLICE), BF16),
            pltpu.VMEM((SLICE, HEAD), BF16),
            pltpu.VMEM((GRID * GRID, 16, 2 * TOK), BF16),
            pltpu.VMEM((8, SLICE), F32),
            pltpu.VMEM((PROWS, SLICE), F32),
            pltpu.VMEM((SECTIONS, 2 * TOK, HEAD), BF16),
            dma((LAYERS, BLOCKS)), dma((LAYERS, 7)), dma((LAYERS, GRID, 3)), dma((LAYERS, GRID * GRID)),
            dma((wide,)), dma((SECTIONS,)), dma((2,)), dma((wide, GRID)), dma((wide, 3)), dma((wide, GRID)),
            dma((wide, 3)), dma((wide,)), dma((wide,)),
            dma((SECTIONS,)), dma((SECTIONS,)), dma((wide, SECTIONS)), dma((wide, SECTIONS)),
            dma((wide, SECTIONS)), dma((wide, SECTIONS)), dma((SECTIONS,)), dma((LAYERS,)), dma((SECTIONS,)), dma((4,)),
        ],
        compiler_params=pltpu.CompilerParams(
            collective_id=0, has_side_effects=True, vmem_limit_bytes=56 * 1024 * 1024
        ),
    )(noise_levels, frame_lengths, latents, kv_weight, mod_shift, mod_scale, mod_gate)


def solution(mesh):
    in_specs = (
        P("stretch", None),
        P(),
        P(),
        P("section", None, None),
        P("section", None, None),
        P("section", None, None),
        P("section", None, None),
    )
    out_specs = P("section", "stretch", None)
    return jax.shard_map(shards, mesh=mesh, in_specs=in_specs, out_specs=out_specs, check_vma=False)
```

```python
import math

import jax
import jax.numpy as jnp
from jax import lax
from jax.experimental import pallas as pl
from jax.experimental.pallas import tpu as pltpu
from jax.sharding import PartitionSpec as P

HEAD = 128
TOK = 128
GRID = 4
SECTIONS = 4
LAYERS = 4
BLOCKS = 2 * GRID * GRID
D = 3072
SLICE = D // SECTIONS
GROUP = SLICE // HEAD
KVW = SECTIONS * HEAD
PIECE = SLICE // (GRID * GRID)
PROWS = TOK + 16
MESH = pl.DeviceIdType.MESH
QSCALE = math.log2(math.e) / math.sqrt(HEAD)
F32 = jnp.float32
BF16 = jnp.bfloat16


def split_two(row):
    high = row.astype(BF16).astype(F32)
    return high, row - high


def stack_rows(rows, width):
    index = lax.broadcasted_iota(jnp.int32, (16, width), 0)
    out = jnp.zeros((16, width), F32)
    for i, row in enumerate(rows):
        out = jnp.where(index == i, row, out)
    return out


def kernel(levels, lengths, latents, weight, shift_tab, scale_tab, gate_tab, out,
           kvbuf, wbuf, w0buf, ybuf, psend, pbuf, statbuf, mods_own, mods, hbuf, qbuf, maskbuf, mbuf, accbuf, sbuf, kv0,
           s_kvr, s_kvown, s_kvrelay, s_kvsib, s_wzr, s_wzs, s_wloc, s_w1r, s_w1s, s_w2r, s_w2s, s_w3r, s_w3s,
           s_mods, s_modr, s_sts, s_str, s_ps, s_pr, s_kv0, s_outs, s_outr, s_w0):
    c = lax.axis_index("stretch")
    s = lax.axis_index("section")
    core = lax.rem(c, 2)
    chip = c // 2
    x = chip // GRID
    y = lax.rem(chip, GRID)

    def device(xx, yy, kk):
        return (xx * GRID + yy) * 2 + kk

    def remote(src, dst, send, recv, stretch, section):
        return pltpu.make_async_remote_copy(src_ref=src, dst_ref=dst, send_sem=send, recv_sem=recv,
                                            device_id=(stretch, section), device_id_type=MESH)

    def arrived(ref, sem):
        pltpu.make_async_copy(ref, ref, sem).wait()

    barrier = pltpu.get_barrier_semaphore()
    partners = []
    for d in range(1, 4):
        partners.append((c, lax.rem(s + d, SECTIONS)))
        partners.append((device(lax.rem(x + d, GRID), y, core), s))
        partners.append((device(x, lax.rem(y + d, GRID), core), s))
    partners.append((device(x, y, 1 - core), s))
    for partner in partners:
        pl.semaphore_signal(barrier, inc=1, device_id=partner, device_id_type=MESH)

    @pl.when(s == 0)
    def _():
        for i in range(4):
            rows = pl.ds(i * SLICE, SLICE)
            pltpu.make_async_copy(weight.at[0, rows], w0buf.at[rows], s_w0.at[i]).start()

    wown = lax.max(s - 1, 0)

    def own_weight(half):
        return pltpu.make_async_copy(
            weight.at[0, pl.ds(pl.multiple_of(s * SLICE, SLICE), SLICE), pl.ds(half * KVW, KVW)],
            wbuf.at[wown, half], s_wloc.at[half])

    @pl.when(s > 0)
    def _():
        own_weight(0).start()
        own_weight(1).start()

    level = levels[c]
    mods_own[0:1, :] = 1.0 + scale_tab[0, pl.ds(level, 1), :]
    mods_own[1:2, :] = shift_tab[0, pl.ds(level, 1), :]
    mods_own[2:3, :] = gate_tab[0, pl.ds(level, 1), :]
    mods_own[3:8, :] = jnp.zeros((5, D), F32)
    for t in range(SECTIONS):
        @pl.when(s == t)
        def _(t=t):
            mods[t] = mods_own[:, t * SLICE:(t + 1) * SLICE]

    def mods_copy(t):
        return remote(mods_own.at[:, pl.ds(t * SLICE, SLICE)], mods.at[s], s_mods.at[t], s_modr.at[s], c, t)

    line = jnp.where(core == 0, y * GRID + x, x * GRID + y)
    line_start = jnp.where(core == 0, y * GRID, x * GRID)
    piece_rows = pl.ds(pl.multiple_of(line * PIECE, PIECE), PIECE)

    def wz_copy(t):
        rows = pl.ds(pl.multiple_of(t * SLICE + line * PIECE, PIECE), PIECE)
        columns = pl.ds(pl.multiple_of(core * KVW, KVW), KVW)
        return remote(weight.at[0, rows, columns], wbuf.at[wown, core, piece_rows], s_wzs.at[t], s_wzr.at[wown], c, t)

    def along_a(d):
        return device(jnp.where(core == 0, lax.rem(x + d, GRID), x), jnp.where(core == 0, y, lax.rem(y + d, GRID)), core)

    def along_b(d):
        return device(jnp.where(core == 0, x, lax.rem(x + d, GRID)), jnp.where(core == 0, lax.rem(y + d, GRID), y), core)

    place_a = jnp.where(core == 0, x, y)
    place_b = jnp.where(core == 0, y, x)
    line_rows = pl.ds(pl.multiple_of(line_start * PIECE, GRID * PIECE), GRID * PIECE)

    def w1_copy(w, d):
        ref = wbuf.at[w, core, piece_rows]
        return remote(ref, ref, s_w1s.at[w, d - 1], s_w1r.at[w, place_a], along_a(d), s)

    def w2_copy(w, d):
        ref = wbuf.at[w, core, line_rows]
        return remote(ref, ref, s_w2s.at[w, d - 1], s_w2r.at[w, place_b], along_b(d), s)

    def w3_copy(w):
        ref = wbuf.at[w, core]
        return remote(ref, ref, s_w3s.at[w], s_w3r.at[w], device(x, y, 1 - core), s)

    def w_step_a(w):
        @pl.when(s != w + 1)
        def _():
            arrived(wbuf.at[w, core, piece_rows], s_wzr.at[w])
            for d in range(1, 4):
                w1_copy(w, d).start()

    def w_step_b(w):
        @pl.when(s != w + 1)
        def _():
            for d in range(1, 4):
                place = lax.rem(place_a + d, GRID)
                rows = pl.ds(pl.multiple_of((line_start + place) * PIECE, PIECE), PIECE)
                arrived(wbuf.at[w, core, rows], s_w1r.at[w, place])
            for d in range(1, 4):
                w2_copy(w, d).start()

    def w_step_c(w):
        @pl.when(s != w + 1)
        def _():
            for d in range(1, 4):
                place = lax.rem(place_b + d, GRID)
                rows = pl.ds(pl.multiple_of(place * GRID * PIECE, GRID * PIECE), GRID * PIECE)
                arrived(wbuf.at[w, core, rows], s_w2r.at[w, place])
            w3_copy(w).start()

    def w_step_d(w):
        @pl.when(s != w + 1)
        def _():
            arrived(wbuf.at[w, 1 - core], s_w3r.at[w])

        @pl.when(s == w + 1)
        def _():
            own_weight(0).wait()
            own_weight(1).wait()

    my_length = lengths[c]

    def finished(keys, values):
        live = lax.broadcasted_iota(jnp.int32, (TOK, HEAD), 0) < my_length
        keys = jnp.where(live, keys, keys[0:1, :]).astype(BF16)
        values = jnp.where(live, values, 0.0)
        return keys, values.T.astype(BF16)

    def store_queries(unit_rows):
        for g in range(GROUP):
            qbuf[g * TOK:(g + 1) * TOK, :] = unit_rows[:, g * HEAD:(g + 1) * HEAD]

    def kv0_copy(t):
        return remote(kv0.at[t], kvbuf.at[0, c], s_kv0.at[t], s_kvr.at[0, c], c, t)

    def greet():
        pl.semaphore_wait(barrier, len(partners))
        for d in range(1, 4):
            t = lax.rem(s + d, SECTIONS)
            mods_copy(t).start()

            @pl.when(s > 0)
            def _(t=t):
                wz_copy(t).start()

    pl.when(s > 0)(greet)
    floats = latents[...].astype(F32)
    row_mean = jnp.mean(floats, axis=-1, keepdims=True)
    row_var = jnp.mean((floats - row_mean) ** 2, axis=-1, keepdims=True)
    row_scale = lax.rsqrt(row_var + 1e-06)

    @pl.when(s == 0)
    def _():
        total = jnp.zeros((TOK, 2 * KVW), F32)
        for i in range(4):
            columns = slice(i * SLICE, (i + 1) * SLICE)
            part = latents[:, columns].astype(F32)
            normed = ((part - row_mean) * row_scale * mods_own[0:1, columns] + mods_own[1:2, columns]).astype(BF16)
            rows = pl.ds(i * SLICE, SLICE)
            pltpu.make_async_copy(weight.at[0, rows], w0buf.at[rows], s_w0.at[i]).wait()
            total = total + jnp.dot(normed, w0buf[i * SLICE:(i + 1) * SLICE, :], preferred_element_type=F32)
        greet()
        for t in (2, 1, 3, 0):
            keys, values = finished(total[:, t * HEAD:(t + 1) * HEAD], total[:, KVW + t * HEAD:KVW + (t + 1) * HEAD])
            if t == 0:
                kvbuf[0, c, 0:TOK, :] = keys
                kvbuf[0, c, TOK:2 * TOK, :] = values
            else:
                kv0[t, 0:TOK, :] = keys
                kv0[t, TOK:2 * TOK, :] = values
                kv0_copy(t).start()

    for w in range(LAYERS - 1):
        w_step_a(w)

    @pl.when(s != 0)
    def _():
        arrived(mods.at[0], s_modr.at[0])

    my_columns = pl.ds(pl.multiple_of(s * SLICE, SLICE), SLICE)
    part = latents[:, my_columns].astype(F32)
    store_queries((((part - row_mean) * row_scale * mods[0, 0:1, :] + mods[0, 1:2, :]) * QSCALE).astype(BF16))

    def mask_step(j, carry):
        lane = lax.broadcasted_iota(jnp.int32, (16, 2 * TOK), 1)
        limit = jnp.where(lane < TOK, lengths[2 * j], lengths[2 * j + 1] + TOK)
        maskbuf[j] = jnp.where(lane < limit, 1.0, 0.0).astype(BF16)
        return carry

    lax.fori_loop(0, GRID * GRID, mask_step, 0)
    w_step_b(0)

    @pl.when(s != 0)
    def _():
        arrived(kvbuf.at[0, c], s_kvr.at[0, c])

    def kv_copy(l, block, sem, stretch):
        ref = kvbuf.at[l, block]
        return remote(ref, ref, sem, s_kvr.at[l, block], stretch, s)

    def act(copy, begin):
        if begin:
            copy.start()
        else:
            copy.wait_send()

    def own_copies(l, begin):
        @pl.when(core == 0)
        def _():
            act(kv_copy(l, c, s_kvown.at[l, 6], device(x, y, 1)), begin)

        for d in (2, 1, 3):
            @pl.when(x + d < GRID)
            def _(d=d):
                act(kv_copy(l, c, s_kvown.at[l, d - 1], device(x + d, y, core)), begin)

            @pl.when((y + d < GRID) | ((core == 1) & (x < GRID - 1)))
            def _(d=d):
                act(kv_copy(l, c, s_kvown.at[l, 2 + d], device(x, lax.rem(y + d, GRID), core)), begin)

    def sibling_copy(l, j):
        return kv_copy(l, 2 * j + core, s_kvsib.at[l, j], device(x, y, 1 - core))

    def own_core_arrived(l, j):
        arrived(kvbuf.at[l, 2 * j + core], s_kvr.at[l, 2 * j + core])

    def column_relays(l, begin):
        def body(xx, carry):
            j = xx * GRID + y
            if begin:
                own_core_arrived(l, j)

            @pl.when(core == 0)
            def _():
                for d in (2, 1, 3):
                    act(kv_copy(l, 2 * j, s_kvrelay.at[l, xx, d - 1], device(x, lax.rem(y + d, GRID), 0)), begin)

            act(sibling_copy(l, j), begin)
            return carry

        lax.fori_loop(0, x, body, 0)

    def row_relays(l, begin, earlier, later):
        for e in (1, 3, 2):
            place = lax.rem(y + e, GRID)
            j = x * GRID + place

            def hand_on(j=j, place=place):
                if begin:
                    own_core_arrived(l, j)

                @pl.when((core == 1) & (x < GRID - 1))
                def _():
                    for d in (2, 1, 3):
                        @pl.when(x + d < GRID)
                        def _(d=d):
                            act(kv_copy(l, 2 * j + 1, s_kvrelay.at[l, place, d - 1], device(x + d, y, 1)), begin)

                @pl.when(place < y)
                def _():
                    act(sibling_copy(l, j), begin)

            if earlier:
                pl.when(place < y)(hand_on)
            if later:
                pl.when((place > y) & (core == 1) & (x < GRID - 1))(hand_on)

    def other_relays(l, xx, begin):
        for e in (1, 3, 2):
            j = xx * GRID + lax.rem(y + e, GRID)
            if begin:
                own_core_arrived(l, j)
            act(sibling_copy(l, j), begin)

    def row_blocks(l, xx, last):
        blocks = []
        for yy in range(GRID):
            first = (xx * GRID + (jnp.minimum(yy, y) if last else yy)) * 2
            second = first + 1
            if last:
                second = jnp.where(yy < y, second, first + core)
            blocks += [(first, yy <= y), (second, (yy < y) | ((yy == y) & (core == 1)))]
        return blocks

    def scores(l, xx, slot, last):
        keys = jnp.concatenate([kvbuf[l, block, 0:TOK] for block, _ in row_blocks(l, xx, last)], axis=0)
        score = lax.dot_general(keys, qbuf[...], (((1,), (1,)), ((), ())), preferred_element_type=F32)
        sbuf[slot] = score
        return jnp.max(score, axis=0, keepdims=True)

    def mix(l, xx, slot, last):
        old_top = mbuf[0:1, :]
        top = mbuf[1:2, :]
        blocks = row_blocks(l, xx, last)
        values = jnp.concatenate([kvbuf[l, block, TOK:] for block, _ in blocks], axis=1)
        masks = jnp.concatenate([maskbuf[xx * GRID + yy] for yy in range(GRID)], axis=1)
        if last:
            lane = lax.broadcasted_iota(jnp.int32, (TOK + 16, 2 * GRID * TOK), 1)
            counted = lane < TOK * (2 * y + 1 + core)
            both = jnp.concatenate([values, masks], axis=0)
            both = jnp.where(counted, both, jnp.zeros_like(both))
        else:
            both = jnp.concatenate([values, masks], axis=0)
        probs = jnp.exp2(sbuf[slot] - top).astype(BF16)
        accbuf[...] = accbuf[...] * jnp.exp2(old_top - top) + jnp.dot(both, probs, preferred_element_type=F32)

    def next_top(found):
        top = mbuf[1:2, :]
        mbuf[0:1, :] = top
        mbuf[1:2, :] = jnp.maximum(top, found)

    def out_columns():
        return pl.ds(pl.multiple_of(s * SLICE, SLICE), SLICE)

    def out_remote(l):
        return remote(hbuf.at[l], out.at[0, :, out_columns()], s_outs.at[l], s_outr.at[s], c, l)

    def out_local(l):
        return pltpu.make_async_copy(hbuf.at[l], out.at[0, :, out_columns()], s_outs.at[l])

    def p_copy(w, t):
        return remote(psend.at[w, t], pbuf.at[w, s], s_ps.at[w, t], s_pr.at[w, s], c, t)

    def stat_copy(w, t):
        ref = statbuf.at[w, s]
        return remote(ref, ref, s_sts.at[w, t], s_str.at[w, s], c, t)

    def layer(l, carry):
        own_copies(l, True)
        mbuf[...] = jnp.full(mbuf.shape, -1e30, F32)
        accbuf[...] = jnp.zeros(accbuf.shape, F32)

        def other_core_arrived(j):
            arrived(kvbuf.at[l, 2 * j + 1 - core], s_kvr.at[l, 2 * j + 1 - core])

        def row_arrived(xx):
            for yy in range(GRID):
                other_core_arrived(xx * GRID + yy)

        def own_row_relays():
            @pl.when(l > 0)
            def _():
                row_relays(l, True, True, True)

        def own_row_arrived():
            lax.fori_loop(x * GRID, chip, lambda j, carry: (other_core_arrived(j), carry)[1], 0)

            @pl.when(core == 1)
            def _():
                arrived(kvbuf.at[l, 2 * chip], s_kvr.at[l, 2 * chip])

        column_relays(l, True)

        @pl.when(l == 0)
        def _():
            row_relays(l, True, True, True)

        for ahead in range(2):
            @pl.when(x > ahead)
            def _(ahead=ahead):
                other_relays(l, ahead, True)

        pl.when(x < 2)(own_row_relays)

        for slot in range(2):
            @pl.when((x > 0) & (lax.rem(x, 2) == 1 - slot))
            def _(slot=slot):
                row_arrived(0)
                next_top(scores(l, 0, slot, False))

        @pl.when(x == 0)
        def _():
            own_row_arrived()
            next_top(scores(l, 0, 1, True))

        for t in range(GRID - 1):
            @pl.when(x + t >= GRID - 1)
            def _(t=t):
                row = x + t - (GRID - 1)
                if t == 0:
                    other_relays(l, row + 2, True)
                if t == 1:
                    own_row_relays()
                if t < 2:
                    row_arrived(row + 1)
                else:
                    own_row_arrived()
                found = scores(l, row + 1, (t + 1) % 2, t == GRID - 2)
                mix(l, row, t % 2, False)
                next_top(found)

        @pl.when(l < LAYERS - 1)
        def _():
            w_step_c(l)

        @pl.when(l < LAYERS - 2)
        def _():
            w_step_b(l + 1)

        mix(l, x, 1, True)

        inverse = 1.0 / accbuf[TOK:TOK + 1, :]
        for g in range(GROUP):
            columns = slice(g * HEAD, (g + 1) * HEAD)
            attended = (accbuf[0:TOK, g * TOK:(g + 1) * TOK] * inverse[:, g * TOK:(g + 1) * TOK]).T

            @pl.when(l == 0)
            def _(g=g, columns=columns):
                start = pl.ds(pl.multiple_of(s * SLICE + g * HEAD, HEAD), HEAD)
                hbuf[0, :, columns] = latents[:, start]

            @pl.when(l > 0)
            def _(columns=columns):
                hbuf[l, :, columns] = hbuf[lax.max(l - 1, 0), :, columns]

            gate = mods[l, 2:3, columns]
            hbuf[l, :, columns] = (hbuf[l, :, columns].astype(F32) + gate * attended).astype(BF16)

        @pl.when(l < LAYERS - 1)
        def _():
            w = l
            hidden = hbuf[l].astype(F32)
            mean = jnp.mean(hidden, axis=-1, keepdims=True)
            centred = hidden - mean
            square = jnp.sum(centred * centred, axis=-1, keepdims=True)
            lane = lax.broadcasted_iota(jnp.int32, (TOK, HEAD), 1)
            tile = jnp.where(lane == 0, mean, jnp.where(lane == 1, square, 0.0)).T
            statbuf[w, s] = tile[0:8, :]
            for d in (2, 1, 3):
                stat_copy(w, lax.rem(s + d, SECTIONS)).start()

            @pl.when(s != l + 1)
            def _():
                arrived(mods.at[l + 1], s_modr.at[l + 1])

            gain = mods[l + 1, 0:1, :]
            shift = mods[l + 1, 1:2, :]
            ybuf[0:TOK, :] = (centred * gain).astype(BF16)
            ybuf[TOK:PROWS, :] = stack_rows(split_two(gain) + split_two(shift), SLICE).astype(BF16)
            w_step_d(w)
            halves = [jnp.dot(ybuf[...], wbuf[w, i], preferred_element_type=F32) for i in range(2)]
            for i in range(2):
                extra = halves[i][TOK:PROWS]
                extra = stack_rows(split_two(extra[0:1] + extra[1:2]) + split_two(extra[2:3] + extra[3:4]), KVW)
                halves[i] = jnp.concatenate([halves[i][0:TOK], extra], axis=0).astype(BF16)
            for t in range(SECTIONS):
                for i in range(2):
                    psend[w, t, :, i * HEAD:(i + 1) * HEAD] = halves[i][:, t * HEAD:(t + 1) * HEAD]
            for d in (2, 1, 3):
                p_copy(w, lax.rem(s + d, SECTIONS)).start()

        @pl.when(l < LAYERS - 1)
        def _():
            w = l
            for d in range(1, 4):
                t = lax.rem(s + d, SECTIONS)
                arrived(statbuf.at[w, t], s_str.at[w, t])
            stats = jnp.concatenate([statbuf[w, t] for t in range(SECTIONS)] + [jnp.zeros((TOK - 8 * SECTIONS, HEAD), F32)], axis=0).T
            means = [stats[:, 8 * t:8 * t + 1] for t in range(SECTIONS)]
            squares = [stats[:, 8 * t + 1:8 * t + 2] for t in range(SECTIONS)]
            mean = sum(means) / SECTIONS
            offsets = [m - mean for m in means]
            variance = sum(sq + SLICE * o * o for sq, o in zip(squares, offsets)) / D
            scale = lax.rsqrt(variance + 1e-06)
            gain = mods[l + 1, 0:1, :]
            shift = mods[l + 1, 1:2, :]
            store_queries((((hbuf[l].astype(F32) - mean) * scale * gain + shift) * QSCALE).astype(BF16))
            pbuf[w, s] = psend[w, s]
            for d in range(1, 4):
                t = lax.rem(s + d, SECTIONS)
                arrived(pbuf.at[w, t], s_pr.at[w, t])
            total = jnp.zeros((TOK, 2 * HEAD), F32)
            bias = jnp.zeros((1, 2 * HEAD), F32)
            for t in range(SECTIONS):
                extra = pbuf[w, t, TOK:PROWS, :].astype(F32)
                total = total + pbuf[w, t, 0:TOK, :].astype(F32) + offsets[t] * (extra[0:1] + extra[1:2])
                bias = bias + extra[2:3] + extra[3:4]
            total = total * scale + bias
            keys, values = finished(total[:, 0:HEAD], total[:, HEAD:])
            kvbuf[l + 1, c, 0:TOK, :] = keys
            kvbuf[l + 1, c, TOK:2 * TOK, :] = values

        @pl.when(s != l)
        def _():
            out_remote(l).start()

        @pl.when(s == l)
        def _():
            out_local(l).start()

        return carry

    lax.fori_loop(0, LAYERS, layer, 0)

    def layer_sent(l, carry):
        own_copies(l, False)

        column_relays(l, False)
        row_relays(l, False, True, True)

        def row(xx, carry):
            other_relays(l, xx, False)
            return carry

        lax.fori_loop(0, x, row, 0)

        @pl.when(s != l)
        def _():
            out_remote(l).wait_send()

        return carry

    lax.fori_loop(0, LAYERS, layer_sent, 0)
    out_local(s).wait()
    for d in range(1, 4):
        t = lax.rem(s + d, SECTIONS)
        mods_copy(t).wait_send()

        @pl.when(s > 0)
        def _(t=t):
            wz_copy(t).wait_send()

    @pl.when(s == 0)
    def _():
        for t in range(1, SECTIONS):
            kv0_copy(t).wait_send()

    def plane_sent(w, carry):
        for d in range(1, 4):
            t = lax.rem(s + d, SECTIONS)
            stat_copy(w, t).wait_send()
            p_copy(w, t).wait_send()

        @pl.when(s != w + 1)
        def _():
            for d in range(1, 4):
                w1_copy(w, d).wait_send()
                w2_copy(w, d).wait_send()
            w3_copy(w).wait_send()

        return carry

    lax.fori_loop(0, LAYERS - 1, plane_sent, 0)
    for d in range(1, 4):
        t = lax.rem(s + d, SECTIONS)
        arrived(out.at[0, :, pl.ds(pl.multiple_of(t * SLICE, SLICE), SLICE)], s_outr.at[t])


def shards(latents, noise_levels, frame_lengths, kv_weight, mod_shift, mod_scale, mod_gate):
    dma = pltpu.SemaphoreType.DMA
    smem = pl.BlockSpec(memory_space=pltpu.SMEM)
    vmem = pl.BlockSpec(memory_space=pltpu.VMEM)
    anywhere = pl.BlockSpec(memory_space=pl.ANY)
    wide = LAYERS - 1
    return pl.pallas_call(
        kernel,
        out_shape=jax.ShapeDtypeStruct((1, TOK, D), BF16),
        in_specs=[smem, smem, vmem, anywhere, vmem, vmem, vmem],
        out_specs=anywhere,
        scratch_shapes=[
            pltpu.VMEM((LAYERS, BLOCKS, 2 * TOK, HEAD), BF16),
            pltpu.VMEM((wide, 2, SLICE, KVW), BF16),
            pltpu.VMEM((D, 2 * KVW), BF16),
            pltpu.VMEM((PROWS, SLICE), BF16),
            pltpu.VMEM((wide, SECTIONS, PROWS, 2 * HEAD), BF16),
            pltpu.VMEM((wide, SECTIONS, PROWS, 2 * HEAD), BF16),
            pltpu.VMEM((wide, SECTIONS, 8, HEAD), F32),
            pltpu.VMEM((8, D), F32),
            pltpu.VMEM((LAYERS, 8, SLICE), F32),
            pltpu.VMEM((LAYERS, TOK, SLICE), BF16),
            pltpu.VMEM((SLICE, HEAD), BF16),
            pltpu.VMEM((GRID * GRID, 16, 2 * TOK), BF16),
            pltpu.VMEM((8, SLICE), F32),
            pltpu.VMEM((PROWS, SLICE), F32),
            pltpu.VMEM((2, 2 * GRID * TOK, SLICE), F32),
            pltpu.VMEM((SECTIONS, 2 * TOK, HEAD), BF16),
            dma((LAYERS, BLOCKS)), dma((LAYERS, 7)), dma((LAYERS, GRID, 3)), dma((LAYERS, GRID * GRID)),
            dma((wide,)), dma((SECTIONS,)), dma((2,)), dma((wide, GRID)), dma((wide, 3)), dma((wide, GRID)),
            dma((wide, 3)), dma((wide,)), dma((wide,)),
            dma((SECTIONS,)), dma((SECTIONS,)), dma((wide, SECTIONS)), dma((wide, SECTIONS)),
            dma((wide, SECTIONS)), dma((wide, SECTIONS)), dma((SECTIONS,)), dma((LAYERS,)), dma((SECTIONS,)), dma((4,)),
        ],
        compiler_params=pltpu.CompilerParams(
            collective_id=0, has_side_effects=True, vmem_limit_bytes=56 * 1024 * 1024
        ),
    )(noise_levels, frame_lengths, latents, kv_weight, mod_shift, mod_scale, mod_gate)


def solution(mesh):
    in_specs = (
        P("stretch", None),
        P(),
        P(),
        P("section", None, None),
        P("section", None, None),
        P("section", None, None),
        P("section", None, None),
    )
    out_specs = P("section", "stretch", None)
    return jax.shard_map(shards, mesh=mesh, in_specs=in_specs, out_specs=out_specs, check_vma=False)
```

```python
import math

import jax
import jax.numpy as jnp
from jax import lax
from jax.experimental import pallas as pl
from jax.experimental.pallas import tpu as pltpu
from jax.sharding import PartitionSpec as P

HEAD = 128
TOK = 128
GRID = 4
SECTIONS = 4
LAYERS = 4
BLOCKS = 2 * GRID * GRID
D = 3072
SLICE = D // SECTIONS
GROUP = SLICE // HEAD
KVW = SECTIONS * HEAD
PIECE = SLICE // (GRID * GRID)
PROWS = TOK + 16
MESH = pl.DeviceIdType.MESH
QSCALE = math.log2(math.e) / math.sqrt(HEAD)
F32 = jnp.float32
BF16 = jnp.bfloat16


def split_two(row):
    high = row.astype(BF16).astype(F32)
    return high, row - high


def stack_rows(rows, width):
    index = lax.broadcasted_iota(jnp.int32, (16, width), 0)
    out = jnp.zeros((16, width), F32)
    for i, row in enumerate(rows):
        out = jnp.where(index == i, row, out)
    return out


def kernel(levels, lengths, latents_in, weight, shift_in, scale_in, gate_in, out,
           latents, tables, kvbuf, wbuf, w0buf, ybuf, psend, pbuf, statbuf, mods_own, mods, hbuf, qbuf, maskbuf, mbuf, accbuf, sbuf, kv0,
           s_kvr, s_kvown, s_kvsib, s_wzr, s_wzs, s_wloc, s_w1r, s_w1s, s_w2r, s_w2s, s_w3r, s_w3s,
           s_mods, s_modr, s_sts, s_str, s_ps, s_pr, s_kv0, s_outs, s_outr, s_w0, s_in):
    c = lax.axis_index("stretch")
    s = lax.axis_index("section")
    core = lax.rem(c, 2)
    chip = c // 2
    x = chip // GRID
    y = lax.rem(chip, GRID)

    def device(xx, yy, kk):
        return (xx * GRID + yy) * 2 + kk

    def remote(src, dst, send, recv, stretch, section):
        return pltpu.make_async_remote_copy(src_ref=src, dst_ref=dst, send_sem=send, recv_sem=recv,
                                            device_id=(stretch, section), device_id_type=MESH)

    def arrived(ref, sem):
        pltpu.make_async_copy(ref, ref, sem).wait()

    inputs = [pltpu.make_async_copy(shift_in.at[0], tables.at[0], s_in.at[0]),
              pltpu.make_async_copy(scale_in.at[0], tables.at[1], s_in.at[1]),
              pltpu.make_async_copy(gate_in.at[0], tables.at[2], s_in.at[2]),
              pltpu.make_async_copy(latents_in, latents, s_in.at[3])]
    for copy in inputs:
        copy.start()

    barrier = pltpu.get_barrier_semaphore()
    for d in range(1, SECTIONS):
        pl.semaphore_signal(barrier, inc=1, device_id=(c, lax.rem(s + d, SECTIONS)), device_id_type=MESH)
    pl.semaphore_signal(barrier, inc=1, device_id=(device(x, y, 1 - core), s), device_id_type=MESH)

    def greet_chip(d, carry):
        other = lax.rem(chip + d, GRID * GRID)
        pl.semaphore_signal(barrier, inc=1, device_id=(2 * other + core, s), device_id_type=MESH)
        return carry

    lax.fori_loop(1, GRID * GRID, greet_chip, 0)

    @pl.when(s == 0)
    def _():
        for i in range(4):
            rows = pl.ds(i * SLICE, SLICE)
            pltpu.make_async_copy(weight.at[0, rows], w0buf.at[rows], s_w0.at[i]).start()

    wown = lax.max(s - 1, 0)

    def own_weight(half):
        return pltpu.make_async_copy(
            weight.at[0, pl.ds(pl.multiple_of(s * SLICE, SLICE), SLICE), pl.ds(half * KVW, KVW)],
            wbuf.at[wown, half], s_wloc.at[half])

    @pl.when(s > 0)
    def _():
        own_weight(0).start()
        own_weight(1).start()

    level = levels[c]
    for copy in inputs[:3]:
        copy.wait()
    mods_own[0:1, :] = 1.0 + tables[1, pl.ds(level, 1), :]
    mods_own[1:2, :] = tables[0, pl.ds(level, 1), :]
    mods_own[2:3, :] = tables[2, pl.ds(level, 1), :]
    mods_own[3:8, :] = jnp.zeros((5, D), F32)
    for t in range(SECTIONS):
        @pl.when(s == t)
        def _(t=t):
            mods[t] = mods_own[:, t * SLICE:(t + 1) * SLICE]

    def mods_copy(t):
        return remote(mods_own.at[:, pl.ds(t * SLICE, SLICE)], mods.at[s], s_mods.at[t], s_modr.at[s], c, t)

    line = jnp.where(core == 0, y * GRID + x, x * GRID + y)
    line_start = jnp.where(core == 0, y * GRID, x * GRID)
    piece_rows = pl.ds(pl.multiple_of(line * PIECE, PIECE), PIECE)

    def wz_copy(t):
        rows = pl.ds(pl.multiple_of(t * SLICE + line * PIECE, PIECE), PIECE)
        columns = pl.ds(pl.multiple_of(core * KVW, KVW), KVW)
        return remote(weight.at[0, rows, columns], wbuf.at[wown, core, piece_rows], s_wzs.at[t], s_wzr.at[wown], c, t)

    def along_a(d):
        return device(jnp.where(core == 0, lax.rem(x + d, GRID), x), jnp.where(core == 0, y, lax.rem(y + d, GRID)), core)

    def along_b(d):
        return device(jnp.where(core == 0, x, lax.rem(x + d, GRID)), jnp.where(core == 0, lax.rem(y + d, GRID), y), core)

    place_a = jnp.where(core == 0, x, y)
    place_b = jnp.where(core == 0, y, x)
    line_rows = pl.ds(pl.multiple_of(line_start * PIECE, GRID * PIECE), GRID * PIECE)

    def w1_copy(w, d):
        ref = wbuf.at[w, core, piece_rows]
        return remote(ref, ref, s_w1s.at[w, d - 1], s_w1r.at[w, place_a], along_a(d), s)

    def w2_copy(w, d):
        ref = wbuf.at[w, core, line_rows]
        return remote(ref, ref, s_w2s.at[w, d - 1], s_w2r.at[w, place_b], along_b(d), s)

    def w3_copy(w):
        ref = wbuf.at[w, core]
        return remote(ref, ref, s_w3s.at[w], s_w3r.at[w], device(x, y, 1 - core), s)

    def w_step_a(w):
        @pl.when(s != w + 1)
        def _():
            arrived(wbuf.at[w, core, piece_rows], s_wzr.at[w])
            for d in range(1, 4):
                w1_copy(w, d).start()

    def w_step_b(w):
        @pl.when(s != w + 1)
        def _():
            for d in range(1, 4):
                place = lax.rem(place_a + d, GRID)
                rows = pl.ds(pl.multiple_of((line_start + place) * PIECE, PIECE), PIECE)
                arrived(wbuf.at[w, core, rows], s_w1r.at[w, place])
            for d in range(1, 4):
                w2_copy(w, d).start()

    def w_step_c(w):
        @pl.when(s != w + 1)
        def _():
            for d in range(1, 4):
                place = lax.rem(place_b + d, GRID)
                rows = pl.ds(pl.multiple_of(place * GRID * PIECE, GRID * PIECE), GRID * PIECE)
                arrived(wbuf.at[w, core, rows], s_w2r.at[w, place])
            w3_copy(w).start()

    def w_step_d(w):
        @pl.when(s != w + 1)
        def _():
            arrived(wbuf.at[w, 1 - core], s_w3r.at[w])

        @pl.when(s == w + 1)
        def _():
            own_weight(0).wait()
            own_weight(1).wait()

    my_length = lengths[c]

    def finished(keys, values):
        live = lax.broadcasted_iota(jnp.int32, (TOK, HEAD), 0) < my_length
        keys = jnp.where(live, keys, keys[0:1, :]).astype(BF16)
        values = jnp.where(live, values, 0.0)
        return keys, values.T.astype(BF16)

    def store_queries(unit_rows):
        for g in range(GROUP):
            qbuf[g * TOK:(g + 1) * TOK, :] = unit_rows[:, g * HEAD:(g + 1) * HEAD]

    def kv0_copy(t):
        return remote(kv0.at[t], kvbuf.at[0, c], s_kv0.at[t], s_kvr.at[0, c], c, t)

    def greet():
        pl.semaphore_wait(barrier, SECTIONS + GRID * GRID - 1)
        for d in range(1, 4):
            t = lax.rem(s + d, SECTIONS)
            mods_copy(t).start()

            @pl.when(s > 0)
            def _(t=t):
                wz_copy(t).start()

    pl.when(s > 0)(greet)
    inputs[3].wait()
    floats = latents[...].astype(F32)
    row_mean = jnp.mean(floats, axis=-1, keepdims=True)
    row_var = jnp.mean((floats - row_mean) ** 2, axis=-1, keepdims=True)
    row_scale = lax.rsqrt(row_var + 1e-06)

    @pl.when(s == 0)
    def _():
        total = jnp.zeros((TOK, 2 * KVW), F32)
        for i in range(4):
            columns = slice(i * SLICE, (i + 1) * SLICE)
            part = latents[:, columns].astype(F32)
            normed = ((part - row_mean) * row_scale * mods_own[0:1, columns] + mods_own[1:2, columns]).astype(BF16)
            rows = pl.ds(i * SLICE, SLICE)
            pltpu.make_async_copy(weight.at[0, rows], w0buf.at[rows], s_w0.at[i]).wait()
            total = total + jnp.dot(normed, w0buf[i * SLICE:(i + 1) * SLICE, :], preferred_element_type=F32)
        greet()
        for t in (2, 1, 3, 0):
            keys, values = finished(total[:, t * HEAD:(t + 1) * HEAD], total[:, KVW + t * HEAD:KVW + (t + 1) * HEAD])
            if t == 0:
                kvbuf[0, c, 0:TOK, :] = keys
                kvbuf[0, c, TOK:2 * TOK, :] = values
            else:
                kv0[t, 0:TOK, :] = keys
                kv0[t, TOK:2 * TOK, :] = values
                kv0_copy(t).start()

    for w in range(LAYERS - 1):
        w_step_a(w)

    @pl.when(s != 0)
    def _():
        arrived(mods.at[0], s_modr.at[0])

    my_columns = pl.ds(pl.multiple_of(s * SLICE, SLICE), SLICE)
    hbuf[0] = latents[:, my_columns]
    part = hbuf[0].astype(F32)
    store_queries((((part - row_mean) * row_scale * mods[0, 0:1, :] + mods[0, 1:2, :]) * QSCALE).astype(BF16))

    def mask_step(j, carry):
        lane = lax.broadcasted_iota(jnp.int32, (16, 2 * TOK), 1)
        limit = jnp.where(lane < TOK, lengths[2 * j], lengths[2 * j + 1] + TOK)
        maskbuf[j] = jnp.where(lane < limit, 1.0, 0.0).astype(BF16)
        return carry

    lax.fori_loop(0, GRID * GRID, mask_step, 0)

    @pl.when(s != 0)
    def _():
        w_step_b(0)
        arrived(kvbuf.at[0, c], s_kvr.at[0, c])

    def kv_copy(l, block, sem, stretch):
        ref = kvbuf.at[l, block]
        return remote(ref, ref, sem, s_kvr.at[l, block], stretch, s)

    def act(copy, begin):
        if begin:
            copy.start()
        else:
            copy.wait_send()

    def own_copies(l, begin):
        @pl.when(core == 0)
        def _():
            act(kv_copy(l, c, s_kvown.at[l, chip], device(x, y, 1)), begin)

        def body(other, carry):
            act(kv_copy(l, c, s_kvown.at[l, other], 2 * other + core), begin)
            return carry

        lax.fori_loop(chip + 1, GRID * GRID, body, 0)

    def hand_over(l, start, stop, begin):
        def body(j, carry):
            block = 2 * j + core
            if begin:
                arrived(kvbuf.at[l, block], s_kvr.at[l, block])
            act(kv_copy(l, block, s_kvsib.at[l, j], device(x, y, 1 - core)), begin)
            return carry

        lax.fori_loop(start, stop, body, 0)

    def row_blocks(l, xx, last):
        blocks = []
        for yy in range(GRID):
            first = (xx * GRID + (jnp.minimum(yy, y) if last else yy)) * 2
            second = first + 1
            if last:
                second = jnp.where(yy < y, second, first + core)
            blocks += [(first, yy <= y), (second, (yy < y) | ((yy == y) & (core == 1)))]
        return blocks

    def scores(l, xx, slot, last):
        keys = jnp.concatenate([kvbuf[l, block, 0:TOK] for block, _ in row_blocks(l, xx, last)], axis=0)
        score = lax.dot_general(keys, qbuf[...], (((1,), (1,)), ((), ())), preferred_element_type=F32)
        sbuf[slot] = score
        return jnp.max(score, axis=0, keepdims=True)

    def mix(l, xx, slot, last):
        old_top = mbuf[0:1, :]
        top = mbuf[1:2, :]
        blocks = row_blocks(l, xx, last)
        values = jnp.concatenate([kvbuf[l, block, TOK:] for block, _ in blocks], axis=1)
        masks = jnp.concatenate([maskbuf[xx * GRID + yy] for yy in range(GRID)], axis=1)
        if last:
            lane = lax.broadcasted_iota(jnp.int32, (TOK + 16, 2 * GRID * TOK), 1)
            counted = lane < TOK * (2 * y + 1 + core)
            both = jnp.concatenate([values, masks], axis=0)
            both = jnp.where(counted, both, jnp.zeros_like(both))
        else:
            both = jnp.concatenate([values, masks], axis=0)
        probs = jnp.exp2(sbuf[slot] - top).astype(BF16)
        accbuf[...] = accbuf[...] * jnp.exp2(old_top - top) + jnp.dot(both, probs, preferred_element_type=F32)

    def next_top(found):
        top = mbuf[1:2, :]
        mbuf[0:1, :] = top
        mbuf[1:2, :] = jnp.maximum(top, found)

    def out_columns():
        return pl.ds(pl.multiple_of(s * SLICE, SLICE), SLICE)

    def out_remote(l):
        return remote(hbuf.at[l + 1], out.at[0, :, out_columns()], s_outs.at[l], s_outr.at[s], c, l)

    def out_local(l):
        return pltpu.make_async_copy(hbuf.at[l + 1], out.at[0, :, out_columns()], s_outs.at[l])

    def p_copy(w, t):
        return remote(psend.at[w, t], pbuf.at[w, s], s_ps.at[w, t], s_pr.at[w, s], c, t)

    def stat_copy(w, t):
        ref = statbuf.at[w, s]
        return remote(ref, ref, s_sts.at[w, t], s_str.at[w, s], c, t)

    def layer(l, carry):
        own_copies(l, True)

        @pl.when((l == 0) & (s == 0))
        def _():
            w_step_b(0)

        mbuf[...] = jnp.full(mbuf.shape, -1e30, F32)
        accbuf[...] = jnp.zeros(accbuf.shape, F32)

        def other_core_arrived(j):
            arrived(kvbuf.at[l, 2 * j + 1 - core], s_kvr.at[l, 2 * j + 1 - core])

        def row_arrived(xx):
            for yy in range(GRID):
                other_core_arrived(xx * GRID + yy)

        def own_row_arrived():
            lax.fori_loop(x * GRID, chip, lambda j, carry: (other_core_arrived(j), carry)[1], 0)

            @pl.when(core == 1)
            def _():
                arrived(kvbuf.at[l, 2 * chip], s_kvr.at[l, 2 * chip])

        hand_over(l, 0, jnp.minimum(chip, 2 * GRID), True)

        for slot in range(2):
            @pl.when((x > 0) & (lax.rem(x, 2) == 1 - slot))
            def _(slot=slot):
                row_arrived(0)
                next_top(scores(l, 0, slot, False))

        @pl.when(x == 0)
        def _():
            own_row_arrived()
            next_top(scores(l, 0, 1, True))

        for t in range(GRID - 1):
            @pl.when(x + t >= GRID - 1)
            def _(t=t):
                row = x + t - (GRID - 1)
                if t < 2:
                    hand_over(l, (row + 2) * GRID, jnp.minimum((row + 3) * GRID, chip), True)
                if t < 2:
                    row_arrived(row + 1)
                else:
                    pl.when(l < LAYERS - 1)(lambda: w_step_c(l))
                    own_row_arrived()
                found = scores(l, row + 1, (t + 1) % 2, t == GRID - 2)
                mix(l, row, t % 2, False)
                next_top(found)

        @pl.when((l < LAYERS - 1) & (x == 0))
        def _():
            w_step_c(l)

        @pl.when(l < LAYERS - 2)
        def _():
            w_step_b(l + 1)

        mix(l, x, 1, True)

        inverse = 1.0 / accbuf[TOK:TOK + 1, :]
        for g in range(GROUP):
            columns = slice(g * HEAD, (g + 1) * HEAD)
            attended = (accbuf[0:TOK, g * TOK:(g + 1) * TOK] * inverse[:, g * TOK:(g + 1) * TOK]).T

            gate = mods[l, 2:3, columns]
            hbuf[l + 1, :, columns] = (hbuf[l, :, columns].astype(F32) + gate * attended).astype(BF16)

        @pl.when(l < LAYERS - 1)
        def _():
            w = l
            hidden = hbuf[l + 1].astype(F32)
            mean = jnp.mean(hidden, axis=-1, keepdims=True)
            centred = hidden - mean
            square = jnp.sum(centred * centred, axis=-1, keepdims=True)
            lane = lax.broadcasted_iota(jnp.int32, (TOK, HEAD), 1)
            tile = jnp.where(lane == 0, mean, jnp.where(lane == 1, square, 0.0)).T
            statbuf[w, s] = tile[0:8, :]
            for d in (2, 1, 3):
                stat_copy(w, lax.rem(s + d, SECTIONS)).start()

            @pl.when(s != l + 1)
            def _():
                arrived(mods.at[l + 1], s_modr.at[l + 1])

            gain = mods[l + 1, 0:1, :]
            shift = mods[l + 1, 1:2, :]
            ybuf[0:TOK, :] = (centred * gain).astype(BF16)
            ybuf[TOK:PROWS, :] = stack_rows(split_two(gain) + split_two(shift), SLICE).astype(BF16)
            w_step_d(w)
            halves = [jnp.dot(ybuf[...], wbuf[w, i], preferred_element_type=F32) for i in range(2)]
            for i in range(2):
                extra = halves[i][TOK:PROWS]
                extra = stack_rows(split_two(extra[0:1] + extra[1:2]) + split_two(extra[2:3] + extra[3:4]), KVW)
                halves[i] = jnp.concatenate([halves[i][0:TOK], extra], axis=0).astype(BF16)
            for t in range(SECTIONS):
                for i in range(2):
                    psend[w, t, :, i * HEAD:(i + 1) * HEAD] = halves[i][:, t * HEAD:(t + 1) * HEAD]
            for d in (2, 1, 3):
                p_copy(w, lax.rem(s + d, SECTIONS)).start()

        @pl.when(l < LAYERS - 1)
        def _():
            w = l
            for d in range(1, 4):
                t = lax.rem(s + d, SECTIONS)
                arrived(statbuf.at[w, t], s_str.at[w, t])
            stats = jnp.concatenate([statbuf[w, t] for t in range(SECTIONS)] + [jnp.zeros((TOK - 8 * SECTIONS, HEAD), F32)], axis=0).T
            means = [stats[:, 8 * t:8 * t + 1] for t in range(SECTIONS)]
            squares = [stats[:, 8 * t + 1:8 * t + 2] for t in range(SECTIONS)]
            mean = sum(means) / SECTIONS
            offsets = [m - mean for m in means]
            variance = sum(sq + SLICE * o * o for sq, o in zip(squares, offsets)) / D
            scale = lax.rsqrt(variance + 1e-06)
            gain = mods[l + 1, 0:1, :]
            shift = mods[l + 1, 1:2, :]
            store_queries((((hbuf[l + 1].astype(F32) - mean) * scale * gain + shift) * QSCALE).astype(BF16))
            pbuf[w, s] = psend[w, s]
            for d in range(1, 4):
                t = lax.rem(s + d, SECTIONS)
                arrived(pbuf.at[w, t], s_pr.at[w, t])
            total = jnp.zeros((TOK, 2 * HEAD), F32)
            bias = jnp.zeros((1, 2 * HEAD), F32)
            for t in range(SECTIONS):
                extra = pbuf[w, t, TOK:PROWS, :].astype(F32)
                total = total + pbuf[w, t, 0:TOK, :].astype(F32) + offsets[t] * (extra[0:1] + extra[1:2])
                bias = bias + extra[2:3] + extra[3:4]
            total = total * scale + bias
            keys, values = finished(total[:, 0:HEAD], total[:, HEAD:])
            kvbuf[l + 1, c, 0:TOK, :] = keys
            kvbuf[l + 1, c, TOK:2 * TOK, :] = values

        @pl.when(s != l)
        def _():
            out_remote(l).start()

        @pl.when(s == l)
        def _():
            out_local(l).start()

        return carry

    lax.fori_loop(0, LAYERS, layer, 0)

    def layer_sent(l, carry):
        own_copies(l, False)

        hand_over(l, 0, chip, False)

        @pl.when(s != l)
        def _():
            out_remote(l).wait_send()

        return carry

    lax.fori_loop(0, LAYERS, layer_sent, 0)
    out_local(s).wait()
    for d in range(1, 4):
        t = lax.rem(s + d, SECTIONS)
        mods_copy(t).wait_send()

        @pl.when(s > 0)
        def _(t=t):
            wz_copy(t).wait_send()

    @pl.when(s == 0)
    def _():
        for t in range(1, SECTIONS):
            kv0_copy(t).wait_send()

    def plane_sent(w, carry):
        for d in range(1, 4):
            t = lax.rem(s + d, SECTIONS)
            stat_copy(w, t).wait_send()
            p_copy(w, t).wait_send()

        @pl.when(s != w + 1)
        def _():
            for d in range(1, 4):
                w1_copy(w, d).wait_send()
                w2_copy(w, d).wait_send()
            w3_copy(w).wait_send()

        return carry

    lax.fori_loop(0, LAYERS - 1, plane_sent, 0)
    for d in range(1, 4):
        t = lax.rem(s + d, SECTIONS)
        arrived(out.at[0, :, pl.ds(pl.multiple_of(t * SLICE, SLICE), SLICE)], s_outr.at[t])


def shards(latents, noise_levels, frame_lengths, kv_weight, mod_shift, mod_scale, mod_gate):
    dma = pltpu.SemaphoreType.DMA
    smem = pl.BlockSpec(memory_space=pltpu.SMEM)
    anywhere = pl.BlockSpec(memory_space=pl.ANY)
    wide = LAYERS - 1
    return pl.pallas_call(
        kernel,
        out_shape=jax.ShapeDtypeStruct((1, TOK, D), BF16),
        in_specs=[smem, smem, anywhere, anywhere, anywhere, anywhere, anywhere],
        out_specs=anywhere,
        scratch_shapes=[
            pltpu.VMEM((TOK, D), BF16),
            pltpu.VMEM((3, 16, D), F32),
            pltpu.VMEM((LAYERS, BLOCKS, 2 * TOK, HEAD), BF16),
            pltpu.VMEM((wide, 2, SLICE, KVW), BF16),
            pltpu.VMEM((D, 2 * KVW), BF16),
            pltpu.VMEM((PROWS, SLICE), BF16),
            pltpu.VMEM((wide, SECTIONS, PROWS, 2 * HEAD), BF16),
            pltpu.VMEM((wide, SECTIONS, PROWS, 2 * HEAD), BF16),
            pltpu.VMEM((wide, SECTIONS, 8, HEAD), F32),
            pltpu.VMEM((8, D), F32),
            pltpu.VMEM((LAYERS, 8, SLICE), F32),
            pltpu.VMEM((LAYERS + 1, TOK, SLICE), BF16),
            pltpu.VMEM((SLICE, HEAD), BF16),
            pltpu.VMEM((GRID * GRID, 16, 2 * TOK), BF16),
            pltpu.VMEM((8, SLICE), F32),
            pltpu.VMEM((PROWS, SLICE), F32),
            pltpu.VMEM((2, 2 * GRID * TOK, SLICE), F32),
            pltpu.VMEM((SECTIONS, 2 * TOK, HEAD), BF16),
            dma((LAYERS, BLOCKS)), dma((LAYERS, GRID * GRID)), dma((LAYERS, GRID * GRID)),
            dma((wide,)), dma((SECTIONS,)), dma((2,)), dma((wide, GRID)), dma((wide, 3)), dma((wide, GRID)),
            dma((wide, 3)), dma((wide,)), dma((wide,)),
            dma((SECTIONS,)), dma((SECTIONS,)), dma((wide, SECTIONS)), dma((wide, SECTIONS)),
            dma((wide, SECTIONS)), dma((wide, SECTIONS)), dma((SECTIONS,)), dma((LAYERS,)), dma((SECTIONS,)), dma((4,)), dma((4,)),
        ],
        compiler_params=pltpu.CompilerParams(
            collective_id=0, has_side_effects=True, vmem_limit_bytes=56 * 1024 * 1024
        ),
    )(noise_levels, frame_lengths, latents, kv_weight, mod_shift, mod_scale, mod_gate)


def solution(mesh):
    in_specs = (
        P("stretch", None),
        P(),
        P(),
        P("section", None, None),
        P("section", None, None),
        P("section", None, None),
        P("section", None, None),
    )
    out_specs = P("section", "stretch", None)
    return jax.shard_map(shards, mesh=mesh, in_specs=in_specs, out_specs=out_specs, check_vma=False)
```

```python
import math

import jax
import jax.numpy as jnp
from jax import lax
from jax.experimental import pallas as pl
from jax.experimental.pallas import tpu as pltpu
from jax.sharding import PartitionSpec as P

HEAD = 128
TOK = 128
GRID = 4
SECTIONS = 4
LAYERS = 4
BLOCKS = 2 * GRID * GRID
D = 3072
SLICE = D // SECTIONS
GROUP = SLICE // HEAD
KVW = SECTIONS * HEAD
PIECE = SLICE // (GRID * GRID)
PROWS = TOK + 16
MESH = pl.DeviceIdType.MESH
QSCALE = math.log2(math.e) / math.sqrt(HEAD)
F32 = jnp.float32
BF16 = jnp.bfloat16


def split_two(row):
    high = row.astype(BF16).astype(F32)
    return high, row - high


def stack_rows(rows, width):
    index = lax.broadcasted_iota(jnp.int32, (16, width), 0)
    out = jnp.zeros((16, width), F32)
    for i, row in enumerate(rows):
        out = jnp.where(index == i, row, out)
    return out


def kernel(levels, lengths, latents_in, weight, shift_in, scale_in, gate_in, out,
           latents, tables, kvbuf, wbuf, w0buf, ybuf, psend, pbuf, statbuf, mods_own, mods, hbuf, qbuf, maskbuf, mbuf, accbuf, sbuf, kv0,
           s_kvr, s_kvown, s_kvsib, s_wzr, s_wzs, s_wloc, s_w1r, s_w1s, s_w2r, s_w2s, s_w3r, s_w3s,
           s_mods, s_modr, s_sts, s_str, s_ps, s_pr, s_kv0, s_outs, s_outr, s_w0, s_in):
    c = lax.axis_index("stretch")
    s = lax.axis_index("section")
    core = lax.rem(c, 2)
    chip = c // 2
    x = chip // GRID
    y = lax.rem(chip, GRID)

    def device(xx, yy, kk):
        return (xx * GRID + yy) * 2 + kk

    def remote(src, dst, send, recv, stretch, section):
        return pltpu.make_async_remote_copy(src_ref=src, dst_ref=dst, send_sem=send, recv_sem=recv,
                                            device_id=(stretch, section), device_id_type=MESH)

    def arrived(ref, sem):
        pltpu.make_async_copy(ref, ref, sem).wait()

    inputs = [pltpu.make_async_copy(shift_in.at[0], tables.at[0], s_in.at[0]),
              pltpu.make_async_copy(scale_in.at[0], tables.at[1], s_in.at[1]),
              pltpu.make_async_copy(gate_in.at[0], tables.at[2], s_in.at[2]),
              pltpu.make_async_copy(latents_in, latents, s_in.at[3])]
    for copy in inputs:
        copy.start()

    barrier = pltpu.get_barrier_semaphore()
    for d in range(1, SECTIONS):
        pl.semaphore_signal(barrier, inc=1, device_id=(c, lax.rem(s + d, SECTIONS)), device_id_type=MESH)
    pl.semaphore_signal(barrier, inc=1, device_id=(device(x, y, 1 - core), s), device_id_type=MESH)

    def greet_chip(d, carry):
        other = lax.rem(chip + d, GRID * GRID)
        pl.semaphore_signal(barrier, inc=1, device_id=(2 * other + core, s), device_id_type=MESH)
        return carry

    lax.fori_loop(1, GRID * GRID, greet_chip, 0)

    @pl.when(s == 0)
    def _():
        for i in range(4):
            rows = pl.ds(i * SLICE, SLICE)
            pltpu.make_async_copy(weight.at[0, rows], w0buf.at[rows], s_w0.at[i]).start()

    wown = lax.max(s - 1, 0)

    def own_weight(half):
        return pltpu.make_async_copy(
            weight.at[0, pl.ds(pl.multiple_of(s * SLICE, SLICE), SLICE), pl.ds(half * KVW, KVW)],
            wbuf.at[wown, half], s_wloc.at[half])

    @pl.when(s > 0)
    def _():
        own_weight(0).start()
        own_weight(1).start()

    level = levels[c]
    for copy in inputs[:3]:
        copy.wait()
    mods_own[0:1, :] = 1.0 + tables[1, pl.ds(level, 1), :]
    mods_own[1:2, :] = tables[0, pl.ds(level, 1), :]
    mods_own[2:3, :] = tables[2, pl.ds(level, 1), :]
    mods_own[3:8, :] = jnp.zeros((5, D), F32)
    for t in range(SECTIONS):
        @pl.when(s == t)
        def _(t=t):
            mods[t] = mods_own[:, t * SLICE:(t + 1) * SLICE]

    def mods_copy(t):
        return remote(mods_own.at[:, pl.ds(t * SLICE, SLICE)], mods.at[s], s_mods.at[t], s_modr.at[s], c, t)

    line = jnp.where(core == 0, y * GRID + x, x * GRID + y)
    line_start = jnp.where(core == 0, y * GRID, x * GRID)
    piece_rows = pl.ds(pl.multiple_of(line * PIECE, PIECE), PIECE)

    def wz_copy(t):
        rows = pl.ds(pl.multiple_of(t * SLICE + line * PIECE, PIECE), PIECE)
        columns = pl.ds(pl.multiple_of(core * KVW, KVW), KVW)
        return remote(weight.at[0, rows, columns], wbuf.at[wown, core, piece_rows], s_wzs.at[t], s_wzr.at[wown], c, t)

    def along_a(d):
        return device(jnp.where(core == 0, lax.rem(x + d, GRID), x), jnp.where(core == 0, y, lax.rem(y + d, GRID)), core)

    def along_b(d):
        return device(jnp.where(core == 0, x, lax.rem(x + d, GRID)), jnp.where(core == 0, lax.rem(y + d, GRID), y), core)

    place_a = jnp.where(core == 0, x, y)
    place_b = jnp.where(core == 0, y, x)
    line_rows = pl.ds(pl.multiple_of(line_start * PIECE, GRID * PIECE), GRID * PIECE)

    def w1_copy(w, d):
        ref = wbuf.at[w, core, piece_rows]
        return remote(ref, ref, s_w1s.at[w, d - 1], s_w1r.at[w, place_a], along_a(d), s)

    def w2_copy(w, d):
        ref = wbuf.at[w, core, line_rows]
        return remote(ref, ref, s_w2s.at[w, d - 1], s_w2r.at[w, place_b], along_b(d), s)

    def w2_piece(w, place, d):
        ref = wbuf.at[w, core, pl.ds(pl.multiple_of((line_start + place) * PIECE, PIECE), PIECE)]
        return remote(ref, ref, s_w2s.at[w, d - 1], s_w2r.at[w, place_b], along_b(d), s)

    def w3_copy(w):
        ref = wbuf.at[w, core]
        return remote(ref, ref, s_w3s.at[w], s_w3r.at[w], device(x, y, 1 - core), s)

    def w_step_a(w):
        @pl.when(s != w + 1)
        def _():
            arrived(wbuf.at[w, core, piece_rows], s_wzr.at[w])
            for d in range(1, 4):
                w1_copy(w, d).start()
            if isinstance(w, int) and w == 0:
                for d in range(1, 4):
                    w2_piece(w, place_a, d).start()

    def w_step_b(w):
        @pl.when(s != w + 1)
        def _():
            for d in (1, 3, 2):
                place = lax.rem(place_a + d, GRID)
                rows = pl.ds(pl.multiple_of((line_start + place) * PIECE, PIECE), PIECE)
                arrived(wbuf.at[w, core, rows], s_w1r.at[w, place])
                if isinstance(w, int) and w == 0:
                    for e in range(1, 4):
                        w2_piece(w, place, e).start()
            if not (isinstance(w, int) and w == 0):
                for d in range(1, 4):
                    w2_copy(w, d).start()

    def w_step_c(w):
        @pl.when(s != w + 1)
        def _():
            for d in range(1, 4):
                place = lax.rem(place_b + d, GRID)
                rows = pl.ds(pl.multiple_of(place * GRID * PIECE, GRID * PIECE), GRID * PIECE)
                arrived(wbuf.at[w, core, rows], s_w2r.at[w, place])
            w3_copy(w).start()

    def w_step_d(w):
        @pl.when(s != w + 1)
        def _():
            arrived(wbuf.at[w, 1 - core], s_w3r.at[w])

        @pl.when(s == w + 1)
        def _():
            own_weight(0).wait()
            own_weight(1).wait()

    my_length = lengths[c]

    def finished(keys, values):
        live = lax.broadcasted_iota(jnp.int32, (TOK, HEAD), 0) < my_length
        keys = jnp.where(live, keys, keys[0:1, :]).astype(BF16)
        values = jnp.where(live, values, 0.0)
        return keys, values.T.astype(BF16)

    def store_queries(unit_rows):
        for g in range(GROUP):
            qbuf[g * TOK:(g + 1) * TOK, :] = unit_rows[:, g * HEAD:(g + 1) * HEAD]

    def kv0_copy(t):
        return remote(kv0.at[t], kvbuf.at[0, c], s_kv0.at[t], s_kvr.at[0, c], c, t)

    def greet():
        pl.semaphore_wait(barrier, SECTIONS + GRID * GRID - 1)
        for d in range(1, 4):
            t = lax.rem(s + d, SECTIONS)
            mods_copy(t).start()

            @pl.when(s > 0)
            def _(t=t):
                wz_copy(t).start()

    pl.when(s > 0)(greet)
    inputs[3].wait()
    floats = latents[...].astype(F32)
    row_mean = jnp.mean(floats, axis=-1, keepdims=True)
    row_var = jnp.mean((floats - row_mean) ** 2, axis=-1, keepdims=True)
    row_scale = lax.rsqrt(row_var + 1e-06)

    @pl.when(s == 0)
    def _():
        total = jnp.zeros((TOK, 2 * KVW), F32)
        for i in range(4):
            columns = slice(i * SLICE, (i + 1) * SLICE)
            part = latents[:, columns].astype(F32)
            normed = ((part - row_mean) * row_scale * mods_own[0:1, columns] + mods_own[1:2, columns]).astype(BF16)
            rows = pl.ds(i * SLICE, SLICE)
            pltpu.make_async_copy(weight.at[0, rows], w0buf.at[rows], s_w0.at[i]).wait()
            total = total + jnp.dot(normed, w0buf[i * SLICE:(i + 1) * SLICE, :], preferred_element_type=F32)
        greet()
        for t in (2, 1, 3, 0):
            keys, values = finished(total[:, t * HEAD:(t + 1) * HEAD], total[:, KVW + t * HEAD:KVW + (t + 1) * HEAD])
            if t == 0:
                kvbuf[0, c, 0:TOK, :] = keys
                kvbuf[0, c, TOK:2 * TOK, :] = values
            else:
                kv0[t, 0:TOK, :] = keys
                kv0[t, TOK:2 * TOK, :] = values
                kv0_copy(t).start()

    w_step_a(0)

    @pl.when(s != 0)
    def _():
        arrived(mods.at[0], s_modr.at[0])

    my_columns = pl.ds(pl.multiple_of(s * SLICE, SLICE), SLICE)
    hbuf[0] = latents[:, my_columns]
    part = hbuf[0].astype(F32)
    store_queries((((part - row_mean) * row_scale * mods[0, 0:1, :] + mods[0, 1:2, :]) * QSCALE).astype(BF16))

    def mask_step(j, carry):
        lane = lax.broadcasted_iota(jnp.int32, (16, 2 * TOK), 1)
        limit = jnp.where(lane < TOK, lengths[2 * j], lengths[2 * j + 1] + TOK)
        maskbuf[j] = jnp.where(lane < limit, 1.0, 0.0).astype(BF16)
        return carry

    lax.fori_loop(0, GRID * GRID, mask_step, 0)

    @pl.when(s != 0)
    def _():
        w_step_b(0)
        arrived(kvbuf.at[0, c], s_kvr.at[0, c])

    def kv_copy(l, block, sem, stretch):
        ref = kvbuf.at[l, block]
        return remote(ref, ref, sem, s_kvr.at[l, block], stretch, s)

    def act(copy, begin):
        if begin:
            copy.start()
        else:
            copy.wait_send()

    def own_copies(l, begin):
        @pl.when(core == 0)
        def _():
            act(kv_copy(l, c, s_kvown.at[l, chip], device(x, y, 1)), begin)

        def body(other, carry):
            act(kv_copy(l, c, s_kvown.at[l, other], 2 * other + core), begin)
            return carry

        lax.fori_loop(chip + 1, GRID * GRID, body, 0)

    def hand_over(l, start, stop, begin):
        def body(j, carry):
            block = 2 * j + core
            if begin:
                arrived(kvbuf.at[l, block], s_kvr.at[l, block])
            act(kv_copy(l, block, s_kvsib.at[l, j], device(x, y, 1 - core)), begin)
            return carry

        lax.fori_loop(start, stop, body, 0)

    def row_blocks(l, xx, last):
        blocks = []
        for yy in range(GRID):
            first = (xx * GRID + (jnp.minimum(yy, y) if last else yy)) * 2
            second = first + 1
            if last:
                second = jnp.where(yy < y, second, first + core)
            blocks += [(first, yy <= y), (second, (yy < y) | ((yy == y) & (core == 1)))]
        return blocks

    def scores(l, xx, slot, last):
        keys = jnp.concatenate([kvbuf[l, block, 0:TOK] for block, _ in row_blocks(l, xx, last)], axis=0)
        score = lax.dot_general(keys, qbuf[...], (((1,), (1,)), ((), ())), preferred_element_type=F32)
        sbuf[slot] = score
        return jnp.max(score, axis=0, keepdims=True)

    def mix(l, xx, slot, last):
        old_top = mbuf[0:1, :]
        top = mbuf[1:2, :]
        blocks = row_blocks(l, xx, last)
        values = jnp.concatenate([kvbuf[l, block, TOK:] for block, _ in blocks], axis=1)
        masks = jnp.concatenate([maskbuf[xx * GRID + yy] for yy in range(GRID)], axis=1)
        if last:
            lane = lax.broadcasted_iota(jnp.int32, (TOK + 16, 2 * GRID * TOK), 1)
            counted = lane < TOK * (2 * y + 1 + core)
            both = jnp.concatenate([values, masks], axis=0)
            both = jnp.where(counted, both, jnp.zeros_like(both))
        else:
            both = jnp.concatenate([values, masks], axis=0)
        probs = jnp.exp2(sbuf[slot] - top).astype(BF16)
        accbuf[...] = accbuf[...] * jnp.exp2(old_top - top) + jnp.dot(both, probs, preferred_element_type=F32)

    def next_top(found):
        top = mbuf[1:2, :]
        mbuf[0:1, :] = top
        mbuf[1:2, :] = jnp.maximum(top, found)

    def out_columns():
        return pl.ds(pl.multiple_of(s * SLICE, SLICE), SLICE)

    def out_remote(l):
        return remote(hbuf.at[l + 1], out.at[0, :, out_columns()], s_outs.at[l], s_outr.at[s], c, l)

    def out_local(l):
        return pltpu.make_async_copy(hbuf.at[l + 1], out.at[0, :, out_columns()], s_outs.at[l])

    def p_copy(w, t):
        return remote(psend.at[w, t], pbuf.at[w, s], s_ps.at[w, t], s_pr.at[w, s], c, t)

    def stat_copy(w, t):
        ref = statbuf.at[w, s]
        return remote(ref, ref, s_sts.at[w, t], s_str.at[w, s], c, t)

    def layer(l, carry):
        own_copies(l, True)

        @pl.when((l == 0) & (s == 0))
        def _():
            w_step_b(0)

        @pl.when(l == 0)
        def _():
            w_step_a(1)
            w_step_a(2)

        mbuf[...] = jnp.full(mbuf.shape, -1e30, F32)
        accbuf[...] = jnp.zeros(accbuf.shape, F32)

        def other_core_arrived(j):
            arrived(kvbuf.at[l, 2 * j + 1 - core], s_kvr.at[l, 2 * j + 1 - core])

        def row_arrived(xx):
            for yy in range(GRID):
                other_core_arrived(xx * GRID + yy)

        def own_row_arrived():
            lax.fori_loop(x * GRID, chip, lambda j, carry: (other_core_arrived(j), carry)[1], 0)

            @pl.when(core == 1)
            def _():
                arrived(kvbuf.at[l, 2 * chip], s_kvr.at[l, 2 * chip])

        hand_over(l, 0, jnp.minimum(chip, 2 * GRID), True)

        for slot in range(2):
            @pl.when((x > 0) & (lax.rem(x, 2) == 1 - slot))
            def _(slot=slot):
                row_arrived(0)
                next_top(scores(l, 0, slot, False))

        @pl.when(x == 0)
        def _():
            own_row_arrived()
            next_top(scores(l, 0, 1, True))

        for t in range(GRID - 1):
            @pl.when(x + t >= GRID - 1)
            def _(t=t):
                row = x + t - (GRID - 1)
                if t < 2:
                    hand_over(l, (row + 2) * GRID, jnp.minimum((row + 3) * GRID, chip), True)
                if t < 2:
                    row_arrived(row + 1)
                else:
                    pl.when(l < LAYERS - 1)(lambda: w_step_c(l))
                    own_row_arrived()
                found = scores(l, row + 1, (t + 1) % 2, t == GRID - 2)
                mix(l, row, t % 2, False)
                next_top(found)

        @pl.when((l < LAYERS - 1) & (x == 0))
        def _():
            w_step_c(l)

        @pl.when(l < LAYERS - 2)
        def _():
            w_step_b(l + 1)

        mix(l, x, 1, True)

        inverse = 1.0 / accbuf[TOK:TOK + 1, :]
        for g in range(GROUP):
            columns = slice(g * HEAD, (g + 1) * HEAD)
            attended = (accbuf[0:TOK, g * TOK:(g + 1) * TOK] * inverse[:, g * TOK:(g + 1) * TOK]).T

            gate = mods[l, 2:3, columns]
            hbuf[l + 1, :, columns] = (hbuf[l, :, columns].astype(F32) + gate * attended).astype(BF16)

        @pl.when(l < LAYERS - 1)
        def _():
            w = l
            hidden = hbuf[l + 1].astype(F32)
            mean = jnp.mean(hidden, axis=-1, keepdims=True)
            centred = hidden - mean
            square = jnp.sum(centred * centred, axis=-1, keepdims=True)
            lane = lax.broadcasted_iota(jnp.int32, (TOK, HEAD), 1)
            tile = jnp.where(lane == 0, mean, jnp.where(lane == 1, square, 0.0)).T
            statbuf[w, s] = tile[0:8, :]
            for d in (2, 1, 3):
                stat_copy(w, lax.rem(s + d, SECTIONS)).start()

            @pl.when(s != l + 1)
            def _():
                arrived(mods.at[l + 1], s_modr.at[l + 1])

            gain = mods[l + 1, 0:1, :]
            shift = mods[l + 1, 1:2, :]
            ybuf[0:TOK, :] = (centred * gain).astype(BF16)
            ybuf[TOK:PROWS, :] = stack_rows(split_two(gain) + split_two(shift), SLICE).astype(BF16)
            w_step_d(w)
            halves = [jnp.dot(ybuf[...], wbuf[w, i], preferred_element_type=F32) for i in range(2)]
            for i in range(2):
                extra = halves[i][TOK:PROWS]
                extra = stack_rows(split_two(extra[0:1] + extra[1:2]) + split_two(extra[2:3] + extra[3:4]), KVW)
                halves[i] = jnp.concatenate([halves[i][0:TOK], extra], axis=0).astype(BF16)
            for t in range(SECTIONS):
                for i in range(2):
                    psend[w, t, :, i * HEAD:(i + 1) * HEAD] = halves[i][:, t * HEAD:(t + 1) * HEAD]
            for d in (2, 1, 3):
                p_copy(w, lax.rem(s + d, SECTIONS)).start()

        @pl.when(l < LAYERS - 1)
        def _():
            w = l
            for d in range(1, 4):
                t = lax.rem(s + d, SECTIONS)
                arrived(statbuf.at[w, t], s_str.at[w, t])
            stats = jnp.concatenate([statbuf[w, t] for t in range(SECTIONS)] + [jnp.zeros((TOK - 8 * SECTIONS, HEAD), F32)], axis=0).T
            means = [stats[:, 8 * t:8 * t + 1] for t in range(SECTIONS)]
            squares = [stats[:, 8 * t + 1:8 * t + 2] for t in range(SECTIONS)]
            mean = sum(means) / SECTIONS
            offsets = [m - mean for m in means]
            variance = sum(sq + SLICE * o * o for sq, o in zip(squares, offsets)) / D
            scale = lax.rsqrt(variance + 1e-06)
            gain = mods[l + 1, 0:1, :]
            shift = mods[l + 1, 1:2, :]
            store_queries((((hbuf[l + 1].astype(F32) - mean) * scale * gain + shift) * QSCALE).astype(BF16))
            pbuf[w, s] = psend[w, s]
            for d in range(1, 4):
                t = lax.rem(s + d, SECTIONS)
                arrived(pbuf.at[w, t], s_pr.at[w, t])
            total = jnp.zeros((TOK, 2 * HEAD), F32)
            bias = jnp.zeros((1, 2 * HEAD), F32)
            for t in range(SECTIONS):
                extra = pbuf[w, t, TOK:PROWS, :].astype(F32)
                total = total + pbuf[w, t, 0:TOK, :].astype(F32) + offsets[t] * (extra[0:1] + extra[1:2])
                bias = bias + extra[2:3] + extra[3:4]
            total = total * scale + bias
            keys, values = finished(total[:, 0:HEAD], total[:, HEAD:])
            kvbuf[l + 1, c, 0:TOK, :] = keys
            kvbuf[l + 1, c, TOK:2 * TOK, :] = values

        @pl.when(s != l)
        def _():
            out_remote(l).start()

        @pl.when(s == l)
        def _():
            out_local(l).start()

        return carry

    lax.fori_loop(0, LAYERS, layer, 0)

    def layer_sent(l, carry):
        own_copies(l, False)

        hand_over(l, 0, chip, False)

        @pl.when(s != l)
        def _():
            out_remote(l).wait_send()

        return carry

    lax.fori_loop(0, LAYERS, layer_sent, 0)
    out_local(s).wait()
    for d in range(1, 4):
        t = lax.rem(s + d, SECTIONS)
        mods_copy(t).wait_send()

        @pl.when(s > 0)
        def _(t=t):
            wz_copy(t).wait_send()

    @pl.when(s == 0)
    def _():
        for t in range(1, SECTIONS):
            kv0_copy(t).wait_send()

    def plane_sent(w, carry):
        for d in range(1, 4):
            t = lax.rem(s + d, SECTIONS)
            stat_copy(w, t).wait_send()
            p_copy(w, t).wait_send()

        @pl.when(s != w + 1)
        def _():
            for d in range(1, 4):
                w1_copy(w, d).wait_send()
                w2_copy(w, d).wait_send()
            w3_copy(w).wait_send()

        return carry

    lax.fori_loop(0, LAYERS - 1, plane_sent, 0)
    for d in range(1, 4):
        t = lax.rem(s + d, SECTIONS)
        arrived(out.at[0, :, pl.ds(pl.multiple_of(t * SLICE, SLICE), SLICE)], s_outr.at[t])


def shards(latents, noise_levels, frame_lengths, kv_weight, mod_shift, mod_scale, mod_gate):
    dma = pltpu.SemaphoreType.DMA
    smem = pl.BlockSpec(memory_space=pltpu.SMEM)
    anywhere = pl.BlockSpec(memory_space=pl.ANY)
    wide = LAYERS - 1
    return pl.pallas_call(
        kernel,
        out_shape=jax.ShapeDtypeStruct((1, TOK, D), BF16),
        in_specs=[smem, smem, anywhere, anywhere, anywhere, anywhere, anywhere],
        out_specs=anywhere,
        scratch_shapes=[
            pltpu.VMEM((TOK, D), BF16),
            pltpu.VMEM((3, 16, D), F32),
            pltpu.VMEM((LAYERS, BLOCKS, 2 * TOK, HEAD), BF16),
            pltpu.VMEM((wide, 2, SLICE, KVW), BF16),
            pltpu.VMEM((D, 2 * KVW), BF16),
            pltpu.VMEM((PROWS, SLICE), BF16),
            pltpu.VMEM((wide, SECTIONS, PROWS, 2 * HEAD), BF16),
            pltpu.VMEM((wide, SECTIONS, PROWS, 2 * HEAD), BF16),
            pltpu.VMEM((wide, SECTIONS, 8, HEAD), F32),
            pltpu.VMEM((8, D), F32),
            pltpu.VMEM((LAYERS, 8, SLICE), F32),
            pltpu.VMEM((LAYERS + 1, TOK, SLICE), BF16),
            pltpu.VMEM((SLICE, HEAD), BF16),
            pltpu.VMEM((GRID * GRID, 16, 2 * TOK), BF16),
            pltpu.VMEM((8, SLICE), F32),
            pltpu.VMEM((PROWS, SLICE), F32),
            pltpu.VMEM((2, 2 * GRID * TOK, SLICE), F32),
            pltpu.VMEM((SECTIONS, 2 * TOK, HEAD), BF16),
            dma((LAYERS, BLOCKS)), dma((LAYERS, GRID * GRID)), dma((LAYERS, GRID * GRID)),
            dma((wide,)), dma((SECTIONS,)), dma((2,)), dma((wide, GRID)), dma((wide, 3)), dma((wide, GRID)),
            dma((wide, 3)), dma((wide,)), dma((wide,)),
            dma((SECTIONS,)), dma((SECTIONS,)), dma((wide, SECTIONS)), dma((wide, SECTIONS)),
            dma((wide, SECTIONS)), dma((wide, SECTIONS)), dma((SECTIONS,)), dma((LAYERS,)), dma((SECTIONS,)), dma((4,)), dma((4,)),
        ],
        compiler_params=pltpu.CompilerParams(
            collective_id=0, has_side_effects=True, vmem_limit_bytes=56 * 1024 * 1024
        ),
    )(noise_levels, frame_lengths, latents, kv_weight, mod_shift, mod_scale, mod_gate)


def solution(mesh):
    in_specs = (
        P("stretch", None),
        P(),
        P(),
        P("section", None, None),
        P("section", None, None),
        P("section", None, None),
        P("section", None, None),
    )
    out_specs = P("section", "stretch", None)
    return jax.shard_map(shards, mesh=mesh, in_specs=in_specs, out_specs=out_specs, check_vma=False)
```

```python
import math

import jax
import jax.numpy as jnp
from jax import lax
from jax.experimental import pallas as pl
from jax.experimental.pallas import tpu as pltpu
from jax.sharding import PartitionSpec as P

HEAD = 128
TOK = 128
GRID = 4
SECTIONS = 4
LAYERS = 4
BLOCKS = 2 * GRID * GRID
D = 3072
SLICE = D // SECTIONS
GROUP = SLICE // HEAD
KVW = SECTIONS * HEAD
PIECE = SLICE // (GRID * GRID)
PROWS = TOK + 16
MESH = pl.DeviceIdType.MESH
QSCALE = math.log2(math.e) / math.sqrt(HEAD)
F32 = jnp.float32
BF16 = jnp.bfloat16


def split_two(row):
    high = row.astype(BF16).astype(F32)
    return high, row - high


def stack_rows(rows, width):
    index = lax.broadcasted_iota(jnp.int32, (16, width), 0)
    out = jnp.zeros((16, width), F32)
    for i, row in enumerate(rows):
        out = jnp.where(index == i, row, out)
    return out


def kernel(levels, lengths, latents_in, weight, shift_in, scale_in, gate_in, out,
           latents, tables, kvbuf, wbuf, w0buf, ybuf, psend, pbuf, statbuf, mods_own, mods, hbuf, qbuf, maskbuf, mbuf, accbuf, sbuf, kv0, rbuf,
           s_kvr, s_kvown, s_kvsib, s_wzr, s_wzs, s_wloc, s_w1r, s_w1s, s_w2r, s_w2s, s_w3r, s_w3s,
           s_mods, s_modr, s_sts, s_str, s_ps, s_pr, s_kv0, s_outs, s_outr, s_w0, s_in, s_half):
    c = lax.axis_index("stretch")
    s = lax.axis_index("section")
    core = lax.rem(c, 2)
    chip = c // 2
    x = chip // GRID
    y = lax.rem(chip, GRID)

    def device(xx, yy, kk):
        return (xx * GRID + yy) * 2 + kk

    def remote(src, dst, send, recv, stretch, section):
        return pltpu.make_async_remote_copy(src_ref=src, dst_ref=dst, send_sem=send, recv_sem=recv,
                                            device_id=(stretch, section), device_id_type=MESH)

    def arrived(ref, sem):
        pltpu.make_async_copy(ref, ref, sem).wait()

    inputs = [pltpu.make_async_copy(shift_in.at[0], tables.at[0], s_in.at[0]),
              pltpu.make_async_copy(scale_in.at[0], tables.at[1], s_in.at[1]),
              pltpu.make_async_copy(gate_in.at[0], tables.at[2], s_in.at[2]),
              pltpu.make_async_copy(latents_in, latents, s_in.at[3])]
    for copy in inputs:
        copy.start()

    barrier = pltpu.get_barrier_semaphore()
    for d in range(1, SECTIONS):
        pl.semaphore_signal(barrier, inc=1, device_id=(c, lax.rem(s + d, SECTIONS)), device_id_type=MESH)
    pl.semaphore_signal(barrier, inc=1, device_id=(device(x, y, 1 - core), s), device_id_type=MESH)

    def greet_chip(d, carry):
        other = lax.rem(chip + d, GRID * GRID)
        pl.semaphore_signal(barrier, inc=1, device_id=(2 * other + core, s), device_id_type=MESH)
        return carry

    lax.fori_loop(1, GRID * GRID, greet_chip, 0)

    @pl.when(s == 0)
    def _():
        for i in range(4):
            rows = pl.ds(i * SLICE, SLICE)
            pltpu.make_async_copy(weight.at[0, rows], w0buf.at[rows], s_w0.at[i]).start()

    wown = lax.max(s - 1, 0)

    def own_weight(half):
        return pltpu.make_async_copy(
            weight.at[0, pl.ds(pl.multiple_of(s * SLICE, SLICE), SLICE), pl.ds(half * KVW, KVW)],
            wbuf.at[wown, half], s_wloc.at[half])

    @pl.when(s > 0)
    def _():
        own_weight(0).start()
        own_weight(1).start()

    level = levels[c]
    for copy in inputs[:3]:
        copy.wait()
    mods_own[0:1, :] = 1.0 + tables[1, pl.ds(level, 1), :]
    mods_own[1:2, :] = tables[0, pl.ds(level, 1), :]
    mods_own[2:3, :] = tables[2, pl.ds(level, 1), :]
    mods_own[3:8, :] = jnp.zeros((5, D), F32)
    for t in range(SECTIONS):
        @pl.when(s == t)
        def _(t=t):
            mods[t] = mods_own[:, t * SLICE:(t + 1) * SLICE]

    def mods_copy(t):
        return remote(mods_own.at[:, pl.ds(t * SLICE, SLICE)], mods.at[s], s_mods.at[t], s_modr.at[s], c, t)

    line = jnp.where(core == 0, y * GRID + x, x * GRID + y)
    line_start = jnp.where(core == 0, y * GRID, x * GRID)
    piece_rows = pl.ds(pl.multiple_of(line * PIECE, PIECE), PIECE)

    def wz_copy(t):
        rows = pl.ds(pl.multiple_of(t * SLICE + line * PIECE, PIECE), PIECE)
        columns = pl.ds(pl.multiple_of(core * KVW, KVW), KVW)
        return remote(weight.at[0, rows, columns], wbuf.at[wown, core, piece_rows], s_wzs.at[t], s_wzr.at[wown], c, t)

    def along_a(d):
        return device(jnp.where(core == 0, lax.rem(x + d, GRID), x), jnp.where(core == 0, y, lax.rem(y + d, GRID)), core)

    def along_b(d):
        return device(jnp.where(core == 0, x, lax.rem(x + d, GRID)), jnp.where(core == 0, lax.rem(y + d, GRID), y), core)

    place_a = jnp.where(core == 0, x, y)
    place_b = jnp.where(core == 0, y, x)
    line_rows = pl.ds(pl.multiple_of(line_start * PIECE, GRID * PIECE), GRID * PIECE)

    def w1_copy(w, d):
        ref = wbuf.at[w, core, piece_rows]
        return remote(ref, ref, s_w1s.at[w, d - 1], s_w1r.at[w, place_a], along_a(d), s)

    def w2_copy(w, d):
        ref = wbuf.at[w, core, line_rows]
        return remote(ref, ref, s_w2s.at[w, d - 1], s_w2r.at[w, place_b], along_b(d), s)

    def w2_piece(w, place, d):
        ref = wbuf.at[w, core, pl.ds(pl.multiple_of((line_start + place) * PIECE, PIECE), PIECE)]
        return remote(ref, ref, s_w2s.at[w, d - 1], s_w2r.at[w, place_b], along_b(d), s)

    def w3_copy(w):
        ref = wbuf.at[w, core]
        return remote(ref, ref, s_w3s.at[w], s_w3r.at[w], device(x, y, 1 - core), s)

    def w_step_a(w):
        @pl.when(s != w + 1)
        def _():
            arrived(wbuf.at[w, core, piece_rows], s_wzr.at[w])
            for d in range(1, 4):
                w1_copy(w, d).start()
            if isinstance(w, int) and w == 0:
                for d in range(1, 4):
                    w2_piece(w, place_a, d).start()

    def w_step_b(w):
        @pl.when(s != w + 1)
        def _():
            for d in (1, 3, 2):
                place = lax.rem(place_a + d, GRID)
                rows = pl.ds(pl.multiple_of((line_start + place) * PIECE, PIECE), PIECE)
                arrived(wbuf.at[w, core, rows], s_w1r.at[w, place])
                if isinstance(w, int) and w == 0:
                    for e in range(1, 4):
                        w2_piece(w, place, e).start()
            if not (isinstance(w, int) and w == 0):
                for d in range(1, 4):
                    w2_copy(w, d).start()

    def w_step_c(w):
        @pl.when(s != w + 1)
        def _():
            for d in range(1, 4):
                place = lax.rem(place_b + d, GRID)
                rows = pl.ds(pl.multiple_of(place * GRID * PIECE, GRID * PIECE), GRID * PIECE)
                arrived(wbuf.at[w, core, rows], s_w2r.at[w, place])
            w3_copy(w).start()

    def w_step_d(w):
        @pl.when(s != w + 1)
        def _():
            arrived(wbuf.at[w, 1 - core], s_w3r.at[w])

        @pl.when(s == w + 1)
        def _():
            own_weight(0).wait()
            own_weight(1).wait()

    my_length = lengths[c]

    def finished(keys, values):
        live = lax.broadcasted_iota(jnp.int32, (TOK, HEAD), 0) < my_length
        keys = jnp.where(live, keys, keys[0:1, :]).astype(BF16)
        values = jnp.where(live, values, 0.0)
        return keys, values.T.astype(BF16)

    def store_queries(unit_rows):
        for g in range(GROUP):
            qbuf[g * TOK:(g + 1) * TOK, :] = unit_rows[:, g * HEAD:(g + 1) * HEAD]

    def kv0_copy(t):
        return remote(kv0.at[t], kvbuf.at[0, c], s_kv0.at[t], s_kvr.at[0, c], c, t)

    def greet():
        pl.semaphore_wait(barrier, SECTIONS + GRID * GRID - 1)
        for d in range(1, 4):
            t = lax.rem(s + d, SECTIONS)
            mods_copy(t).start()

            @pl.when(s > 0)
            def _(t=t):
                wz_copy(t).start()

    pl.when(s > 0)(greet)
    inputs[3].wait()
    floats = latents[...].astype(F32)
    row_mean = jnp.mean(floats, axis=-1, keepdims=True)
    row_var = jnp.mean((floats - row_mean) ** 2, axis=-1, keepdims=True)
    row_scale = lax.rsqrt(row_var + 1e-06)

    @pl.when(s == 0)
    def _():
        total = jnp.zeros((TOK, 2 * KVW), F32)
        for i in range(4):
            columns = slice(i * SLICE, (i + 1) * SLICE)
            part = latents[:, columns].astype(F32)
            normed = ((part - row_mean) * row_scale * mods_own[0:1, columns] + mods_own[1:2, columns]).astype(BF16)
            rows = pl.ds(i * SLICE, SLICE)
            pltpu.make_async_copy(weight.at[0, rows], w0buf.at[rows], s_w0.at[i]).wait()
            total = total + jnp.dot(normed, w0buf[i * SLICE:(i + 1) * SLICE, :], preferred_element_type=F32)
        greet()
        for t in (2, 1, 3, 0):
            keys, values = finished(total[:, t * HEAD:(t + 1) * HEAD], total[:, KVW + t * HEAD:KVW + (t + 1) * HEAD])
            if t == 0:
                kvbuf[0, c, 0:TOK, :] = keys
                kvbuf[0, c, TOK:2 * TOK, :] = values
            else:
                kv0[t, 0:TOK, :] = keys
                kv0[t, TOK:2 * TOK, :] = values
                kv0_copy(t).start()

    w_step_a(0)

    @pl.when(s != 0)
    def _():
        arrived(mods.at[0], s_modr.at[0])

    my_columns = pl.ds(pl.multiple_of(s * SLICE, SLICE), SLICE)
    hbuf[0] = latents[:, my_columns]
    part = hbuf[0].astype(F32)
    store_queries((((part - row_mean) * row_scale * mods[0, 0:1, :] + mods[0, 1:2, :]) * QSCALE).astype(BF16))

    def mask_step(j, carry):
        lane = lax.broadcasted_iota(jnp.int32, (16, 2 * TOK), 1)
        limit = jnp.where(lane < TOK, lengths[2 * j], lengths[2 * j + 1] + TOK)
        maskbuf[j] = jnp.where(lane < limit, 1.0, 0.0).astype(BF16)
        return carry

    lax.fori_loop(0, GRID * GRID, mask_step, 0)

    @pl.when(s != 0)
    def _():
        w_step_b(0)
        arrived(kvbuf.at[0, c], s_kvr.at[0, c])

    def kv_copy(l, block, sem, stretch):
        ref = kvbuf.at[l, block]
        return remote(ref, ref, sem, s_kvr.at[l, block], stretch, s)

    def act(copy, begin):
        if begin:
            copy.start()
        else:
            copy.wait_send()

    def own_copies(l, begin):
        @pl.when(core == 0)
        def _():
            act(kv_copy(l, c, s_kvown.at[l, chip], device(x, y, 1)), begin)

        def body(other, carry):
            act(kv_copy(l, c, s_kvown.at[l, other], 2 * other + core), begin)
            return carry

        lax.fori_loop(chip + 1, GRID * GRID, body, 0)

    def hand_over(l, start, stop, begin):
        def body(j, carry):
            block = 2 * j + core
            if begin:
                arrived(kvbuf.at[l, block], s_kvr.at[l, block])
            act(kv_copy(l, block, s_kvsib.at[l, j], device(x, y, 1 - core)), begin)
            return carry

        lax.fori_loop(start, stop, body, 0)

    def row_blocks(l, xx, last):
        blocks = []
        for yy in range(GRID):
            first = (xx * GRID + (jnp.minimum(yy, y) if last else yy)) * 2
            second = first + 1
            if last:
                second = jnp.where(yy < y, second, first + core)
            blocks += [(first, yy <= y), (second, (yy < y) | ((yy == y) & (core == 1)))]
        return blocks

    def scores(l, xx, slot, last):
        keys = jnp.concatenate([kvbuf[l, block, 0:TOK] for block, _ in row_blocks(l, xx, last)], axis=0)
        score = lax.dot_general(keys, qbuf[...], (((1,), (1,)), ((), ())), preferred_element_type=F32)
        sbuf[slot] = score
        return jnp.max(score, axis=0, keepdims=True)

    def mix(l, xx, slot, last):
        old_top = mbuf[0:1, :]
        top = mbuf[1:2, :]
        blocks = row_blocks(l, xx, last)
        values = jnp.concatenate([kvbuf[l, block, TOK:] for block, _ in blocks], axis=1)
        masks = jnp.concatenate([maskbuf[xx * GRID + yy] for yy in range(GRID)], axis=1)
        if last:
            lane = lax.broadcasted_iota(jnp.int32, (TOK + 16, 2 * GRID * TOK), 1)
            counted = lane < TOK * (2 * y + 1 + core)
            both = jnp.concatenate([values, masks], axis=0)
            both = jnp.where(counted, both, jnp.zeros_like(both))
        else:
            both = jnp.concatenate([values, masks], axis=0)
        probs = jnp.exp2(sbuf[slot] - top).astype(BF16)
        accbuf[...] = accbuf[...] * jnp.exp2(old_top - top) + jnp.dot(both, probs, preferred_element_type=F32)

    def next_top(found):
        top = mbuf[1:2, :]
        mbuf[0:1, :] = top
        mbuf[1:2, :] = jnp.maximum(top, found)

    def out_columns():
        return pl.ds(pl.multiple_of(s * SLICE, SLICE), SLICE)

    def out_remote(l):
        return remote(hbuf.at[l + 1], out.at[0, :, out_columns()], s_outs.at[l], s_outr.at[s], c, l)

    last = LAYERS - 1
    far = (last + 2) % SECTIONS
    sides = ((last + 1) % SECTIONS, last - 1)
    half = TOK // 2

    def half_copy(i):
        return remote(hbuf.at[LAYERS, pl.ds(i * half, half)], rbuf, s_half.at[i], s_half.at[2], c, sides[i])

    def relay_copy(i):
        return remote(rbuf, out.at[0, pl.ds(i * half, half), pl.ds(far * SLICE, SLICE)], s_half.at[3], s_outr.at[far], c, last)

    def out_direct(l):
        return (s != l) & ((l < last) | (s != far))

    def out_local(l):
        return pltpu.make_async_copy(hbuf.at[l + 1], out.at[0, :, out_columns()], s_outs.at[l])

    def p_copy(w, t):
        return remote(psend.at[w, t], pbuf.at[w, s], s_ps.at[w, t], s_pr.at[w, s], c, t)

    def stat_copy(w, t):
        ref = statbuf.at[w, s]
        return remote(ref, ref, s_sts.at[w, t], s_str.at[w, s], c, t)

    def layer(l, carry):
        own_copies(l, True)

        @pl.when((l == 0) & (s == 0))
        def _():
            w_step_b(0)

        @pl.when(l == 0)
        def _():
            w_step_a(1)
            w_step_a(2)

        mbuf[...] = jnp.full(mbuf.shape, -1e30, F32)
        accbuf[...] = jnp.zeros(accbuf.shape, F32)

        def other_core_arrived(j):
            arrived(kvbuf.at[l, 2 * j + 1 - core], s_kvr.at[l, 2 * j + 1 - core])

        def row_arrived(xx):
            for yy in range(GRID):
                other_core_arrived(xx * GRID + yy)

        def own_row_arrived():
            lax.fori_loop(x * GRID, chip, lambda j, carry: (other_core_arrived(j), carry)[1], 0)

            @pl.when(core == 1)
            def _():
                arrived(kvbuf.at[l, 2 * chip], s_kvr.at[l, 2 * chip])

        hand_over(l, 0, jnp.minimum(chip, 2 * GRID), True)

        for slot in range(2):
            @pl.when((x > 0) & (lax.rem(x, 2) == 1 - slot))
            def _(slot=slot):
                row_arrived(0)
                next_top(scores(l, 0, slot, False))

        @pl.when(x == 0)
        def _():
            own_row_arrived()
            next_top(scores(l, 0, 1, True))

        for t in range(GRID - 1):
            @pl.when(x + t >= GRID - 1)
            def _(t=t):
                row = x + t - (GRID - 1)
                if t < 2:
                    hand_over(l, (row + 2) * GRID, jnp.minimum((row + 3) * GRID, chip), True)
                if t < 2:
                    row_arrived(row + 1)
                else:
                    pl.when(l < LAYERS - 1)(lambda: w_step_c(l))
                    own_row_arrived()
                found = scores(l, row + 1, (t + 1) % 2, t == GRID - 2)
                mix(l, row, t % 2, False)
                next_top(found)

        @pl.when((l < LAYERS - 1) & (x == 0))
        def _():
            w_step_c(l)

        @pl.when(l < LAYERS - 2)
        def _():
            w_step_b(l + 1)

        mix(l, x, 1, True)

        inverse = 1.0 / accbuf[TOK:TOK + 1, :]
        for g in range(GROUP):
            columns = slice(g * HEAD, (g + 1) * HEAD)
            attended = (accbuf[0:TOK, g * TOK:(g + 1) * TOK] * inverse[:, g * TOK:(g + 1) * TOK]).T

            gate = mods[l, 2:3, columns]
            hbuf[l + 1, :, columns] = (hbuf[l, :, columns].astype(F32) + gate * attended).astype(BF16)

        @pl.when(l < LAYERS - 1)
        def _():
            w = l
            hidden = hbuf[l + 1].astype(F32)
            mean = jnp.mean(hidden, axis=-1, keepdims=True)
            centred = hidden - mean
            square = jnp.sum(centred * centred, axis=-1, keepdims=True)
            lane = lax.broadcasted_iota(jnp.int32, (TOK, HEAD), 1)
            tile = jnp.where(lane == 0, mean, jnp.where(lane == 1, square, 0.0)).T
            statbuf[w, s] = tile[0:8, :]
            for d in (2, 1, 3):
                stat_copy(w, lax.rem(s + d, SECTIONS)).start()

            @pl.when(s != l + 1)
            def _():
                arrived(mods.at[l + 1], s_modr.at[l + 1])

            gain = mods[l + 1, 0:1, :]
            shift = mods[l + 1, 1:2, :]
            ybuf[0:TOK, :] = (centred * gain).astype(BF16)
            ybuf[TOK:PROWS, :] = stack_rows(split_two(gain) + split_two(shift), SLICE).astype(BF16)
            w_step_d(w)
            halves = [jnp.dot(ybuf[...], wbuf[w, i], preferred_element_type=F32) for i in range(2)]
            for i in range(2):
                extra = halves[i][TOK:PROWS]
                extra = stack_rows(split_two(extra[0:1] + extra[1:2]) + split_two(extra[2:3] + extra[3:4]), KVW)
                halves[i] = jnp.concatenate([halves[i][0:TOK], extra], axis=0).astype(BF16)
            for t in range(SECTIONS):
                for i in range(2):
                    psend[w, t, :, i * HEAD:(i + 1) * HEAD] = halves[i][:, t * HEAD:(t + 1) * HEAD]
            for d in (2, 1, 3):
                p_copy(w, lax.rem(s + d, SECTIONS)).start()

        @pl.when(l < LAYERS - 1)
        def _():
            w = l
            for d in range(1, 4):
                t = lax.rem(s + d, SECTIONS)
                arrived(statbuf.at[w, t], s_str.at[w, t])
            stats = jnp.concatenate([statbuf[w, t] for t in range(SECTIONS)] + [jnp.zeros((TOK - 8 * SECTIONS, HEAD), F32)], axis=0).T
            means = [stats[:, 8 * t:8 * t + 1] for t in range(SECTIONS)]
            squares = [stats[:, 8 * t + 1:8 * t + 2] for t in range(SECTIONS)]
            mean = sum(means) / SECTIONS
            offsets = [m - mean for m in means]
            variance = sum(sq + SLICE * o * o for sq, o in zip(squares, offsets)) / D
            scale = lax.rsqrt(variance + 1e-06)
            gain = mods[l + 1, 0:1, :]
            shift = mods[l + 1, 1:2, :]
            store_queries((((hbuf[l + 1].astype(F32) - mean) * scale * gain + shift) * QSCALE).astype(BF16))
            pbuf[w, s] = psend[w, s]
            for d in range(1, 4):
                t = lax.rem(s + d, SECTIONS)
                arrived(pbuf.at[w, t], s_pr.at[w, t])
            total = jnp.zeros((TOK, 2 * HEAD), F32)
            bias = jnp.zeros((1, 2 * HEAD), F32)
            for t in range(SECTIONS):
                extra = pbuf[w, t, TOK:PROWS, :].astype(F32)
                total = total + pbuf[w, t, 0:TOK, :].astype(F32) + offsets[t] * (extra[0:1] + extra[1:2])
                bias = bias + extra[2:3] + extra[3:4]
            total = total * scale + bias
            keys, values = finished(total[:, 0:HEAD], total[:, HEAD:])
            kvbuf[l + 1, c, 0:TOK, :] = keys
            kvbuf[l + 1, c, TOK:2 * TOK, :] = values

        @pl.when(out_direct(l))
        def _():
            out_remote(l).start()

        @pl.when((l == last) & (s == far))
        def _():
            half_copy(0).start()
            half_copy(1).start()

        @pl.when(s == l)
        def _():
            out_local(l).start()

        return carry

    lax.fori_loop(0, LAYERS, layer, 0)
    for i in range(2):
        @pl.when(s == sides[i])
        def _(i=i):
            arrived(rbuf, s_half.at[2])
            relay_copy(i).start()

    def layer_sent(l, carry):
        own_copies(l, False)

        hand_over(l, 0, chip, False)

        @pl.when(out_direct(l))
        def _():
            out_remote(l).wait_send()

        return carry

    lax.fori_loop(0, LAYERS, layer_sent, 0)
    out_local(s).wait()
    for i in range(2):
        @pl.when(s == sides[i])
        def _(i=i):
            relay_copy(i).wait_send()

        @pl.when(s == far)
        def _(i=i):
            half_copy(i).wait_send()

    for d in range(1, 4):
        t = lax.rem(s + d, SECTIONS)
        mods_copy(t).wait_send()

        @pl.when(s > 0)
        def _(t=t):
            wz_copy(t).wait_send()

    @pl.when(s == 0)
    def _():
        for t in range(1, SECTIONS):
            kv0_copy(t).wait_send()

    def plane_sent(w, carry):
        for d in range(1, 4):
            t = lax.rem(s + d, SECTIONS)
            stat_copy(w, t).wait_send()
            p_copy(w, t).wait_send()

        @pl.when(s != w + 1)
        def _():
            for d in range(1, 4):
                w1_copy(w, d).wait_send()
                w2_copy(w, d).wait_send()
            w3_copy(w).wait_send()

        return carry

    lax.fori_loop(0, LAYERS - 1, plane_sent, 0)
    for d in range(1, 4):
        t = lax.rem(s + d, SECTIONS)
        arrived(out.at[0, :, pl.ds(pl.multiple_of(t * SLICE, SLICE), SLICE)], s_outr.at[t])


def shards(latents, noise_levels, frame_lengths, kv_weight, mod_shift, mod_scale, mod_gate):
    dma = pltpu.SemaphoreType.DMA
    smem = pl.BlockSpec(memory_space=pltpu.SMEM)
    anywhere = pl.BlockSpec(memory_space=pl.ANY)
    wide = LAYERS - 1
    return pl.pallas_call(
        kernel,
        out_shape=jax.ShapeDtypeStruct((1, TOK, D), BF16),
        in_specs=[smem, smem, anywhere, anywhere, anywhere, anywhere, anywhere],
        out_specs=anywhere,
        scratch_shapes=[
            pltpu.VMEM((TOK, D), BF16),
            pltpu.VMEM((3, 16, D), F32),
            pltpu.VMEM((LAYERS, BLOCKS, 2 * TOK, HEAD), BF16),
            pltpu.VMEM((wide, 2, SLICE, KVW), BF16),
            pltpu.VMEM((D, 2 * KVW), BF16),
            pltpu.VMEM((PROWS, SLICE), BF16),
            pltpu.VMEM((wide, SECTIONS, PROWS, 2 * HEAD), BF16),
            pltpu.VMEM((wide, SECTIONS, PROWS, 2 * HEAD), BF16),
            pltpu.VMEM((wide, SECTIONS, 8, HEAD), F32),
            pltpu.VMEM((8, D), F32),
            pltpu.VMEM((LAYERS, 8, SLICE), F32),
            pltpu.VMEM((LAYERS + 1, TOK, SLICE), BF16),
            pltpu.VMEM((SLICE, HEAD), BF16),
            pltpu.VMEM((GRID * GRID, 16, 2 * TOK), BF16),
            pltpu.VMEM((8, SLICE), F32),
            pltpu.VMEM((PROWS, SLICE), F32),
            pltpu.VMEM((2, 2 * GRID * TOK, SLICE), F32),
            pltpu.VMEM((SECTIONS, 2 * TOK, HEAD), BF16),
            pltpu.VMEM((TOK // 2, SLICE), BF16),
            dma((LAYERS, BLOCKS)), dma((LAYERS, GRID * GRID)), dma((LAYERS, GRID * GRID)),
            dma((wide,)), dma((SECTIONS,)), dma((2,)), dma((wide, GRID)), dma((wide, 3)), dma((wide, GRID)),
            dma((wide, 3)), dma((wide,)), dma((wide,)),
            dma((SECTIONS,)), dma((SECTIONS,)), dma((wide, SECTIONS)), dma((wide, SECTIONS)),
            dma((wide, SECTIONS)), dma((wide, SECTIONS)), dma((SECTIONS,)), dma((LAYERS,)), dma((SECTIONS,)), dma((4,)), dma((4,)), dma((4,)),
        ],
        compiler_params=pltpu.CompilerParams(
            collective_id=0, has_side_effects=True, vmem_limit_bytes=56 * 1024 * 1024
        ),
    )(noise_levels, frame_lengths, latents, kv_weight, mod_shift, mod_scale, mod_gate)


def solution(mesh):
    in_specs = (
        P("stretch", None),
        P(),
        P(),
        P("section", None, None),
        P("section", None, None),
        P("section", None, None),
        P("section", None, None),
    )
    out_specs = P("section", "stretch", None)
    return jax.shard_map(shards, mesh=mesh, in_specs=in_specs, out_specs=out_specs, check_vma=False)
```

```python
import math

import jax
import jax.numpy as jnp
from jax import lax
from jax.experimental import pallas as pl
from jax.experimental.pallas import tpu as pltpu
from jax.sharding import PartitionSpec as P

HEAD = 128
TOK = 128
GRID = 4
SECTIONS = 4
LAYERS = 4
BLOCKS = 2 * GRID * GRID
D = 3072
SLICE = D // SECTIONS
GROUP = SLICE // HEAD
KVW = SECTIONS * HEAD
PIECE = SLICE // (GRID * GRID)
PROWS = TOK + 16
MESH = pl.DeviceIdType.MESH
QSCALE = math.log2(math.e) / math.sqrt(HEAD)
F32 = jnp.float32
BF16 = jnp.bfloat16


def split_two(row):
    high = row.astype(BF16).astype(F32)
    return high, row - high


def stack_rows(rows, width):
    index = lax.broadcasted_iota(jnp.int32, (16, width), 0)
    out = jnp.zeros((16, width), F32)
    for i, row in enumerate(rows):
        out = jnp.where(index == i, row, out)
    return out


def kernel(levels, lengths, latents_in, weight, shift_in, scale_in, gate_in, out,
           latents, tables, kvbuf, wbuf, w0buf, ybuf, psend, pbuf, statbuf, mods_own, mods, hbuf, qbuf, maskbuf, mbuf, accbuf, sbuf, kv0, rbuf,
           s_kvr, s_kvown, s_kvsib, s_wzr, s_wzs, s_wloc, s_w1r, s_w1s, s_w2r, s_w2s, s_w3r, s_w3s,
           s_mods, s_modr, s_sts, s_str, s_ps, s_pr, s_kv0, s_outs, s_outr, s_w0, s_in, s_half):
    c = lax.axis_index("stretch")
    s = lax.axis_index("section")
    core = lax.rem(c, 2)
    chip = c // 2
    x = chip // GRID
    y = lax.rem(chip, GRID)

    def device(xx, yy, kk):
        return (xx * GRID + yy) * 2 + kk

    def remote(src, dst, send, recv, stretch, section):
        return pltpu.make_async_remote_copy(src_ref=src, dst_ref=dst, send_sem=send, recv_sem=recv,
                                            device_id=(stretch, section), device_id_type=MESH)

    def arrived(ref, sem):
        pltpu.make_async_copy(ref, ref, sem).wait()

    barrier = pltpu.get_barrier_semaphore()
    for d in range(1, SECTIONS):
        pl.semaphore_signal(barrier, inc=1, device_id=(c, lax.rem(s + d, SECTIONS)), device_id_type=MESH)
    pl.semaphore_signal(barrier, inc=1, device_id=(device(x, y, 1 - core), s), device_id_type=MESH)

    def greet_chip(d, carry):
        other = lax.rem(chip + d, GRID * GRID)
        pl.semaphore_signal(barrier, inc=1, device_id=(2 * other + core, s), device_id_type=MESH)
        return carry

    lax.fori_loop(1, GRID * GRID, greet_chip, 0)

    inputs = [pltpu.make_async_copy(shift_in.at[0], tables.at[0], s_in.at[0]),
              pltpu.make_async_copy(scale_in.at[0], tables.at[1], s_in.at[1]),
              pltpu.make_async_copy(gate_in.at[0], tables.at[2], s_in.at[2]),
              pltpu.make_async_copy(latents_in, latents, s_in.at[3])]
    for copy in inputs:
        copy.start()

    @pl.when(s == 0)
    def _():
        for i in range(4):
            rows = pl.ds(i * SLICE, SLICE)
            pltpu.make_async_copy(weight.at[0, rows], w0buf.at[rows], s_w0.at[i]).start()

    wown = lax.max(s - 1, 0)

    def own_weight(half):
        return pltpu.make_async_copy(
            weight.at[0, pl.ds(pl.multiple_of(s * SLICE, SLICE), SLICE), pl.ds(half * KVW, KVW)],
            wbuf.at[wown, half], s_wloc.at[half])

    @pl.when(s > 0)
    def _():
        own_weight(0).start()
        own_weight(1).start()

    level = levels[c]
    for copy in inputs[:3]:
        copy.wait()
    mods_own[0:1, :] = 1.0 + tables[1, pl.ds(level, 1), :]
    mods_own[1:2, :] = tables[0, pl.ds(level, 1), :]
    mods_own[2:3, :] = tables[2, pl.ds(level, 1), :]
    mods_own[3:8, :] = jnp.zeros((5, D), F32)
    for t in range(SECTIONS):
        @pl.when(s == t)
        def _(t=t):
            mods[t] = mods_own[:, t * SLICE:(t + 1) * SLICE]

    def mods_copy(t):
        return remote(mods_own.at[:, pl.ds(t * SLICE, SLICE)], mods.at[s], s_mods.at[t], s_modr.at[s], c, t)

    line = jnp.where(core == 0, y * GRID + x, x * GRID + y)
    line_start = jnp.where(core == 0, y * GRID, x * GRID)
    piece_rows = pl.ds(pl.multiple_of(line * PIECE, PIECE), PIECE)

    def wz_copy(t):
        rows = pl.ds(pl.multiple_of(t * SLICE + line * PIECE, PIECE), PIECE)
        columns = pl.ds(pl.multiple_of(core * KVW, KVW), KVW)
        return remote(weight.at[0, rows, columns], wbuf.at[wown, core, piece_rows], s_wzs.at[t], s_wzr.at[wown], c, t)

    def along_a(d):
        return device(jnp.where(core == 0, lax.rem(x + d, GRID), x), jnp.where(core == 0, y, lax.rem(y + d, GRID)), core)

    def along_b(d):
        return device(jnp.where(core == 0, x, lax.rem(x + d, GRID)), jnp.where(core == 0, lax.rem(y + d, GRID), y), core)

    place_a = jnp.where(core == 0, x, y)
    place_b = jnp.where(core == 0, y, x)
    line_rows = pl.ds(pl.multiple_of(line_start * PIECE, GRID * PIECE), GRID * PIECE)

    def w1_copy(w, d):
        ref = wbuf.at[w, core, piece_rows]
        return remote(ref, ref, s_w1s.at[w, d - 1], s_w1r.at[w, place_a], along_a(d), s)

    def w2_copy(w, d):
        ref = wbuf.at[w, core, line_rows]
        return remote(ref, ref, s_w2s.at[w, d - 1], s_w2r.at[w, place_b], along_b(d), s)

    def w2_piece(w, place, d):
        ref = wbuf.at[w, core, pl.ds(pl.multiple_of((line_start + place) * PIECE, PIECE), PIECE)]
        return remote(ref, ref, s_w2s.at[w, d - 1], s_w2r.at[w, place_b], along_b(d), s)

    def w3_copy(w):
        ref = wbuf.at[w, core]
        return remote(ref, ref, s_w3s.at[w], s_w3r.at[w], device(x, y, 1 - core), s)

    def w_step_a(w):
        @pl.when(s != w + 1)
        def _():
            arrived(wbuf.at[w, core, piece_rows], s_wzr.at[w])
            for d in range(1, 4):
                w1_copy(w, d).start()
            if isinstance(w, int) and w == 0:
                for d in range(1, 4):
                    w2_piece(w, place_a, d).start()

    def w_step_b(w):
        @pl.when(s != w + 1)
        def _():
            for d in (1, 3, 2):
                place = lax.rem(place_a + d, GRID)
                rows = pl.ds(pl.multiple_of((line_start + place) * PIECE, PIECE), PIECE)
                arrived(wbuf.at[w, core, rows], s_w1r.at[w, place])
                if isinstance(w, int) and w == 0:
                    for e in range(1, 4):
                        w2_piece(w, place, e).start()
            if not (isinstance(w, int) and w == 0):
                for d in range(1, 4):
                    w2_copy(w, d).start()

    def w_step_c(w):
        @pl.when(s != w + 1)
        def _():
            for d in range(1, 4):
                place = lax.rem(place_b + d, GRID)
                rows = pl.ds(pl.multiple_of(place * GRID * PIECE, GRID * PIECE), GRID * PIECE)
                arrived(wbuf.at[w, core, rows], s_w2r.at[w, place])
            w3_copy(w).start()

    def w_step_d(w):
        @pl.when(s != w + 1)
        def _():
            arrived(wbuf.at[w, 1 - core], s_w3r.at[w])

        @pl.when(s == w + 1)
        def _():
            own_weight(0).wait()
            own_weight(1).wait()

    my_length = lengths[c]

    def finished(keys, values):
        live = lax.broadcasted_iota(jnp.int32, (TOK, HEAD), 0) < my_length
        keys = jnp.where(live, keys, keys[0:1, :]).astype(BF16)
        values = jnp.where(live, values, 0.0)
        return keys, values.T.astype(BF16)

    def store_queries(unit_rows):
        for g in range(GROUP):
            qbuf[g * TOK:(g + 1) * TOK, :] = unit_rows[:, g * HEAD:(g + 1) * HEAD]

    def kv0_copy(t):
        return remote(kv0.at[t], kvbuf.at[0, c], s_kv0.at[t], s_kvr.at[0, c], c, t)

    def greet():
        pl.semaphore_wait(barrier, SECTIONS + GRID * GRID - 1)
        for d in range(1, 4):
            t = lax.rem(s + d, SECTIONS)

            @pl.when(s > 0)
            def _(t=t):
                wz_copy(t).start()

            mods_copy(t).start()

    pl.when(s > 0)(greet)
    inputs[3].wait()
    floats = latents[...].astype(F32)
    row_mean = jnp.mean(floats, axis=-1, keepdims=True)
    row_var = jnp.mean((floats - row_mean) ** 2, axis=-1, keepdims=True)
    row_scale = lax.rsqrt(row_var + 1e-06)

    @pl.when(s == 0)
    def _():
        total = jnp.zeros((TOK, 2 * KVW), F32)
        for i in range(4):
            columns = slice(i * SLICE, (i + 1) * SLICE)
            part = latents[:, columns].astype(F32)
            normed = ((part - row_mean) * row_scale * mods_own[0:1, columns] + mods_own[1:2, columns]).astype(BF16)
            rows = pl.ds(i * SLICE, SLICE)
            pltpu.make_async_copy(weight.at[0, rows], w0buf.at[rows], s_w0.at[i]).wait()
            total = total + jnp.dot(normed, w0buf[i * SLICE:(i + 1) * SLICE, :], preferred_element_type=F32)
        greet()
        for t in (2, 1, 3, 0):
            keys, values = finished(total[:, t * HEAD:(t + 1) * HEAD], total[:, KVW + t * HEAD:KVW + (t + 1) * HEAD])
            if t == 0:
                kvbuf[0, c, 0:TOK, :] = keys
                kvbuf[0, c, TOK:2 * TOK, :] = values
            else:
                kv0[t, 0:TOK, :] = keys
                kv0[t, TOK:2 * TOK, :] = values
                kv0_copy(t).start()

    w_step_a(0)

    @pl.when(s != 0)
    def _():
        arrived(mods.at[0], s_modr.at[0])

    my_columns = pl.ds(pl.multiple_of(s * SLICE, SLICE), SLICE)
    hbuf[0] = latents[:, my_columns]
    part = hbuf[0].astype(F32)
    store_queries((((part - row_mean) * row_scale * mods[0, 0:1, :] + mods[0, 1:2, :]) * QSCALE).astype(BF16))

    def mask_step(j, carry):
        lane = lax.broadcasted_iota(jnp.int32, (16, 2 * TOK), 1)
        limit = jnp.where(lane < TOK, lengths[2 * j], lengths[2 * j + 1] + TOK)
        maskbuf[j] = jnp.where(lane < limit, 1.0, 0.0).astype(BF16)
        return carry

    lax.fori_loop(0, GRID * GRID, mask_step, 0)

    @pl.when(s != 0)
    def _():
        w_step_b(0)
        arrived(kvbuf.at[0, c], s_kvr.at[0, c])

    def kv_copy(l, block, sem, stretch):
        ref = kvbuf.at[l, block]
        return remote(ref, ref, sem, s_kvr.at[l, block], stretch, s)

    def act(copy, begin):
        if begin:
            copy.start()
        else:
            copy.wait_send()

    def own_copies(l, begin):
        @pl.when(core == 0)
        def _():
            act(kv_copy(l, c, s_kvown.at[l, chip], device(x, y, 1)), begin)

        def body(other, carry):
            act(kv_copy(l, c, s_kvown.at[l, other], 2 * other + core), begin)
            return carry

        lax.fori_loop(chip + 1, GRID * GRID, body, 0)

    def hand_over(l, start, stop, begin):
        def body(j, carry):
            block = 2 * j + core
            if begin:
                arrived(kvbuf.at[l, block], s_kvr.at[l, block])
            act(kv_copy(l, block, s_kvsib.at[l, j], device(x, y, 1 - core)), begin)
            return carry

        lax.fori_loop(start, stop, body, 0)

    def row_blocks(l, xx, last):
        blocks = []
        for yy in range(GRID):
            first = (xx * GRID + (jnp.minimum(yy, y) if last else yy)) * 2
            second = first + 1
            if last:
                second = jnp.where(yy < y, second, first + core)
            blocks += [(first, yy <= y), (second, (yy < y) | ((yy == y) & (core == 1)))]
        return blocks

    def scores(l, xx, slot, last):
        keys = jnp.concatenate([kvbuf[l, block, 0:TOK] for block, _ in row_blocks(l, xx, last)], axis=0)
        score = lax.dot_general(keys, qbuf[...], (((1,), (1,)), ((), ())), preferred_element_type=F32)
        sbuf[slot] = score
        return jnp.max(score, axis=0, keepdims=True)

    def mix(l, xx, slot, last):
        old_top = mbuf[0:1, :]
        top = mbuf[1:2, :]
        blocks = row_blocks(l, xx, last)
        values = jnp.concatenate([kvbuf[l, block, TOK:] for block, _ in blocks], axis=1)
        masks = jnp.concatenate([maskbuf[xx * GRID + yy] for yy in range(GRID)], axis=1)
        if last:
            lane = lax.broadcasted_iota(jnp.int32, (TOK + 16, 2 * GRID * TOK), 1)
            counted = lane < TOK * (2 * y + 1 + core)
            both = jnp.concatenate([values, masks], axis=0)
            both = jnp.where(counted, both, jnp.zeros_like(both))
        else:
            both = jnp.concatenate([values, masks], axis=0)
        probs = jnp.exp2(sbuf[slot] - top).astype(BF16)
        accbuf[...] = accbuf[...] * jnp.exp2(old_top - top) + jnp.dot(both, probs, preferred_element_type=F32)

    def next_top(found):
        top = mbuf[1:2, :]
        mbuf[0:1, :] = top
        mbuf[1:2, :] = jnp.maximum(top, found)

    def out_columns():
        return pl.ds(pl.multiple_of(s * SLICE, SLICE), SLICE)

    def out_remote(l):
        return remote(hbuf.at[l + 1], out.at[0, :, out_columns()], s_outs.at[l], s_outr.at[s], c, l)

    last = LAYERS - 1
    far = (last + 2) % SECTIONS
    sides = ((last + 1) % SECTIONS, last - 1)
    half = TOK // 2

    def half_copy(i):
        return remote(hbuf.at[LAYERS, pl.ds(i * half, half)], rbuf, s_half.at[i], s_half.at[2], c, sides[i])

    def relay_copy(i):
        return remote(rbuf, out.at[0, pl.ds(i * half, half), pl.ds(far * SLICE, SLICE)], s_half.at[3], s_outr.at[far], c, last)

    def out_direct(l):
        return (s != l) & ((l < last) | (s != far))

    def out_local(l):
        return pltpu.make_async_copy(hbuf.at[l + 1], out.at[0, :, out_columns()], s_outs.at[l])

    def p_copy(w, t):
        return remote(psend.at[w, t], pbuf.at[w, s], s_ps.at[w, t], s_pr.at[w, s], c, t)

    def stat_copy(w, t):
        ref = statbuf.at[w, s]
        return remote(ref, ref, s_sts.at[w, t], s_str.at[w, s], c, t)

    def layer(l, carry):
        own_copies(l, True)

        @pl.when((l == 0) & (s == 0))
        def _():
            w_step_b(0)

        @pl.when(l == 0)
        def _():
            w_step_a(1)
            w_step_a(2)

        mbuf[...] = jnp.full(mbuf.shape, -1e30, F32)
        accbuf[...] = jnp.zeros(accbuf.shape, F32)

        def other_core_arrived(j):
            arrived(kvbuf.at[l, 2 * j + 1 - core], s_kvr.at[l, 2 * j + 1 - core])

        def row_arrived(xx):
            for yy in range(GRID):
                other_core_arrived(xx * GRID + yy)

        def own_row_arrived():
            lax.fori_loop(x * GRID, chip, lambda j, carry: (other_core_arrived(j), carry)[1], 0)

            @pl.when(core == 1)
            def _():
                arrived(kvbuf.at[l, 2 * chip], s_kvr.at[l, 2 * chip])

        hand_over(l, 0, jnp.minimum(chip, 2 * GRID), True)

        for slot in range(2):
            @pl.when((x > 0) & (lax.rem(x, 2) == 1 - slot))
            def _(slot=slot):
                row_arrived(0)
                next_top(scores(l, 0, slot, False))

        @pl.when(x == 0)
        def _():
            own_row_arrived()
            next_top(scores(l, 0, 1, True))

        for t in range(GRID - 1):
            @pl.when(x + t >= GRID - 1)
            def _(t=t):
                row = x + t - (GRID - 1)
                if t < 2:
                    hand_over(l, (row + 2) * GRID, jnp.minimum((row + 3) * GRID, chip), True)
                if t < 2:
                    row_arrived(row + 1)
                else:
                    pl.when(l < LAYERS - 1)(lambda: w_step_c(l))
                    own_row_arrived()
                found = scores(l, row + 1, (t + 1) % 2, t == GRID - 2)
                mix(l, row, t % 2, False)
                next_top(found)

        @pl.when((l < LAYERS - 1) & (x == 0))
        def _():
            w_step_c(l)

        @pl.when(l < LAYERS - 2)
        def _():
            w_step_b(l + 1)

        mix(l, x, 1, True)

        inverse = 1.0 / accbuf[TOK:TOK + 1, :]
        for g in range(GROUP):
            columns = slice(g * HEAD, (g + 1) * HEAD)
            attended = (accbuf[0:TOK, g * TOK:(g + 1) * TOK] * inverse[:, g * TOK:(g + 1) * TOK]).T

            gate = mods[l, 2:3, columns]
            hbuf[l + 1, :, columns] = (hbuf[l, :, columns].astype(F32) + gate * attended).astype(BF16)

        @pl.when(l < LAYERS - 1)
        def _():
            w = l
            hidden = hbuf[l + 1].astype(F32)
            mean = jnp.mean(hidden, axis=-1, keepdims=True)
            centred = hidden - mean
            square = jnp.sum(centred * centred, axis=-1, keepdims=True)
            lane = lax.broadcasted_iota(jnp.int32, (TOK, HEAD), 1)
            tile = jnp.where(lane == 0, mean, jnp.where(lane == 1, square, 0.0)).T
            statbuf[w, s] = tile[0:8, :]
            for d in (2, 1, 3):
                stat_copy(w, lax.rem(s + d, SECTIONS)).start()

            @pl.when(s != l + 1)
            def _():
                arrived(mods.at[l + 1], s_modr.at[l + 1])

            gain = mods[l + 1, 0:1, :]
            shift = mods[l + 1, 1:2, :]
            ybuf[0:TOK, :] = (centred * gain).astype(BF16)
            ybuf[TOK:PROWS, :] = stack_rows(split_two(gain) + split_two(shift), SLICE).astype(BF16)
            w_step_d(w)
            halves = [jnp.dot(ybuf[...], wbuf[w, i], preferred_element_type=F32) for i in range(2)]
            for i in range(2):
                extra = halves[i][TOK:PROWS]
                extra = stack_rows(split_two(extra[0:1] + extra[1:2]) + split_two(extra[2:3] + extra[3:4]), KVW)
                halves[i] = jnp.concatenate([halves[i][0:TOK], extra], axis=0).astype(BF16)
            for t in range(SECTIONS):
                for i in range(2):
                    psend[w, t, :, i * HEAD:(i + 1) * HEAD] = halves[i][:, t * HEAD:(t + 1) * HEAD]
            for d in (2, 1, 3):
                p_copy(w, lax.rem(s + d, SECTIONS)).start()

        @pl.when(l < LAYERS - 1)
        def _():
            w = l
            for d in range(1, 4):
                t = lax.rem(s + d, SECTIONS)
                arrived(statbuf.at[w, t], s_str.at[w, t])
            stats = jnp.concatenate([statbuf[w, t] for t in range(SECTIONS)] + [jnp.zeros((TOK - 8 * SECTIONS, HEAD), F32)], axis=0).T
            means = [stats[:, 8 * t:8 * t + 1] for t in range(SECTIONS)]
            squares = [stats[:, 8 * t + 1:8 * t + 2] for t in range(SECTIONS)]
            mean = sum(means) / SECTIONS
            offsets = [m - mean for m in means]
            variance = sum(sq + SLICE * o * o for sq, o in zip(squares, offsets)) / D
            scale = lax.rsqrt(variance + 1e-06)
            gain = mods[l + 1, 0:1, :]
            shift = mods[l + 1, 1:2, :]
            store_queries((((hbuf[l + 1].astype(F32) - mean) * scale * gain + shift) * QSCALE).astype(BF16))
            pbuf[w, s] = psend[w, s]
            for d in range(1, 4):
                t = lax.rem(s + d, SECTIONS)
                arrived(pbuf.at[w, t], s_pr.at[w, t])
            total = jnp.zeros((TOK, 2 * HEAD), F32)
            bias = jnp.zeros((1, 2 * HEAD), F32)
            for t in range(SECTIONS):
                extra = pbuf[w, t, TOK:PROWS, :].astype(F32)
                total = total + pbuf[w, t, 0:TOK, :].astype(F32) + offsets[t] * (extra[0:1] + extra[1:2])
                bias = bias + extra[2:3] + extra[3:4]
            total = total * scale + bias
            keys, values = finished(total[:, 0:HEAD], total[:, HEAD:])
            kvbuf[l + 1, c, 0:TOK, :] = keys
            kvbuf[l + 1, c, TOK:2 * TOK, :] = values

        @pl.when(out_direct(l))
        def _():
            out_remote(l).start()

        @pl.when((l == last) & (s == far))
        def _():
            half_copy(0).start()
            half_copy(1).start()

        @pl.when(s == l)
        def _():
            out_local(l).start()

        return carry

    lax.fori_loop(0, LAYERS, layer, 0)
    for i in range(2):
        @pl.when(s == sides[i])
        def _(i=i):
            arrived(rbuf, s_half.at[2])
            relay_copy(i).start()

    def layer_sent(l, carry):
        own_copies(l, False)

        hand_over(l, 0, chip, False)

        @pl.when(out_direct(l))
        def _():
            out_remote(l).wait_send()

        return carry

    lax.fori_loop(0, LAYERS, layer_sent, 0)
    out_local(s).wait()
    for i in range(2):
        @pl.when(s == sides[i])
        def _(i=i):
            relay_copy(i).wait_send()

        @pl.when(s == far)
        def _(i=i):
            half_copy(i).wait_send()

    for d in range(1, 4):
        t = lax.rem(s + d, SECTIONS)
        mods_copy(t).wait_send()

        @pl.when(s > 0)
        def _(t=t):
            wz_copy(t).wait_send()

    @pl.when(s == 0)
    def _():
        for t in range(1, SECTIONS):
            kv0_copy(t).wait_send()

    def plane_sent(w, carry):
        for d in range(1, 4):
            t = lax.rem(s + d, SECTIONS)
            stat_copy(w, t).wait_send()
            p_copy(w, t).wait_send()

        @pl.when(s != w + 1)
        def _():
            for d in range(1, 4):
                w1_copy(w, d).wait_send()
                w2_copy(w, d).wait_send()
            w3_copy(w).wait_send()

        return carry

    lax.fori_loop(0, LAYERS - 1, plane_sent, 0)
    for d in range(1, 4):
        t = lax.rem(s + d, SECTIONS)
        arrived(out.at[0, :, pl.ds(pl.multiple_of(t * SLICE, SLICE), SLICE)], s_outr.at[t])


def shards(latents, noise_levels, frame_lengths, kv_weight, mod_shift, mod_scale, mod_gate):
    dma = pltpu.SemaphoreType.DMA
    smem = pl.BlockSpec(memory_space=pltpu.SMEM)
    anywhere = pl.BlockSpec(memory_space=pl.ANY)
    wide = LAYERS - 1
    return pl.pallas_call(
        kernel,
        out_shape=jax.ShapeDtypeStruct((1, TOK, D), BF16),
        in_specs=[smem, smem, anywhere, anywhere, anywhere, anywhere, anywhere],
        out_specs=anywhere,
        scratch_shapes=[
            pltpu.VMEM((TOK, D), BF16),
            pltpu.VMEM((3, 16, D), F32),
            pltpu.VMEM((LAYERS, BLOCKS, 2 * TOK, HEAD), BF16),
            pltpu.VMEM((wide, 2, SLICE, KVW), BF16),
            pltpu.VMEM((D, 2 * KVW), BF16),
            pltpu.VMEM((PROWS, SLICE), BF16),
            pltpu.VMEM((wide, SECTIONS, PROWS, 2 * HEAD), BF16),
            pltpu.VMEM((wide, SECTIONS, PROWS, 2 * HEAD), BF16),
            pltpu.VMEM((wide, SECTIONS, 8, HEAD), F32),
            pltpu.VMEM((8, D), F32),
            pltpu.VMEM((LAYERS, 8, SLICE), F32),
            pltpu.VMEM((LAYERS + 1, TOK, SLICE), BF16),
            pltpu.VMEM((SLICE, HEAD), BF16),
            pltpu.VMEM((GRID * GRID, 16, 2 * TOK), BF16),
            pltpu.VMEM((8, SLICE), F32),
            pltpu.VMEM((PROWS, SLICE), F32),
            pltpu.VMEM((2, 2 * GRID * TOK, SLICE), F32),
            pltpu.VMEM((SECTIONS, 2 * TOK, HEAD), BF16),
            pltpu.VMEM((TOK // 2, SLICE), BF16),
            dma((LAYERS, BLOCKS)), dma((LAYERS, GRID * GRID)), dma((LAYERS, GRID * GRID)),
            dma((wide,)), dma((SECTIONS,)), dma((2,)), dma((wide, GRID)), dma((wide, 3)), dma((wide, GRID)),
            dma((wide, 3)), dma((wide,)), dma((wide,)),
            dma((SECTIONS,)), dma((SECTIONS,)), dma((wide, SECTIONS)), dma((wide, SECTIONS)),
            dma((wide, SECTIONS)), dma((wide, SECTIONS)), dma((SECTIONS,)), dma((LAYERS,)), dma((SECTIONS,)), dma((4,)), dma((4,)), dma((4,)),
        ],
        compiler_params=pltpu.CompilerParams(
            collective_id=0, has_side_effects=True, vmem_limit_bytes=56 * 1024 * 1024
        ),
    )(noise_levels, frame_lengths, latents, kv_weight, mod_shift, mod_scale, mod_gate)


def solution(mesh):
    in_specs = (
        P("stretch", None),
        P(),
        P(),
        P("section", None, None),
        P("section", None, None),
        P("section", None, None),
        P("section", None, None),
    )
    out_specs = P("section", "stretch", None)
    return jax.shard_map(shards, mesh=mesh, in_specs=in_specs, out_specs=out_specs, check_vma=False)
```
